128 devices in a mesh: replica: 16 (over x_lo, z, core), tensor: 8 (over y, x_hi).
Axes of the slice: x: 4 (x_hi: 2, x_lo: 2; x = x_hi * 2 + x_lo), y: 4, z: 4, core: 2. Of those that a mesh axis runs over, the one named last changes fastest.
Arguments:
- first_queries: bfloat16 [256, 8192], P('replica', 'tensor'), may hold values from -100 to 100
- first_key_value: bfloat16 [256, 2, 1024], P('replica', None, 'tensor'), may hold values from -4.5 to 4.5
- second_queries: bfloat16 [256, 8192], P('replica', 'tensor'), may hold values from -100 to 100
- second_key_value: bfloat16 [256, 2, 1024], P('replica', None, 'tensor'), may hold values from -4.5 to 4.5
- key_value_pool: bfloat16 [2048, 64, 2, 1024], P('replica', None, None, 'tensor'), may hold values from -4.5 to 4.5
- request_blocks: int32 [256, 8], replicated, may hold values from 0 to 127, as said below
- lengths: int32 [256], replicated, may hold values from 1 to 511
- moving_request_list: int32 [32], replicated, may hold values from 0 to 15, as said below
- adapter_index: int32 [256], replicated, may hold values from 0 to 1, as said below
- adapter_rank_bucket: int32 [32], replicated, may hold values from 0 to 3
- replica_pair_mask: int32 [1], replicated, may hold values from 1 to 15
- adapter_down_factors: bfloat16 [32, 8192, 128], P('replica', 'tensor'), may hold values from -0.25 to 0.25
- adapter_up_factors: bfloat16 [32, 128, 8192], P('replica', None, 'tensor'), may hold values from -0.5 to 0.5
- output_weight: bfloat16 [8192, 8192], P('tensor'), may hold values from -0.375 to 0.375
Outputs:
- out_first: bfloat16 [256, 8192], P('replica', 'tensor')
- out_second: bfloat16 [256, 8192], P('replica', 'tensor')
- incoming_cache: bfloat16 [32, 512, 2, 1024], P('replica', None, None, 'tensor')
- received_down: bfloat16 [32, 8192, 128], P('replica', 'tensor')
- received_up: bfloat16 [32, 128, 8192], P('replica', None, 'tensor')
The draws below stay inside these ranges and needn't reach their ends.
Inputs may be any that keep to these rules, and one draw needn't show every extreme that they name: `request_blocks`: each replica's rows name distinct blocks of that replica's pool; no block serves two requests. `moving_request_list`: the 2 entries of a replica are distinct requests of that replica. `adapter_index`: the leaving requests of every replica use all 2 of its adapters.
All inputs are finite; a program needn't handle non-finite values.
Results may differ from the reference program's by a relative error of at most 0.019.
Values may be sent and summed in bfloat16 or wider, within the bound.
No kernel may reach another device: no remote copies, remote signals or barrier semaphores. Data moves between devices by JAX's collectives and lax.ppermute only.
A program may use at most 128 MiB of HBM per device.

```python
import jax
import jax.numpy as jnp
from jax import lax

MODEL_WIDTH = 8192
QUERY_HEADS = 64
KEY_VALUE_HEADS = 8
HEAD_WIDTH = 128
PADDED_RANK = 128
REQUEST_COUNT = 16
MOVING_REQUESTS = 2
ADAPTER_COUNT = 2
BLOCK_TOKENS = 64
MAXB = 8
BLOCK_COUNT = 128
N_REPLICA = 16


def shuffle_blocks(sub_key):
    return jax.random.permutation(sub_key, REQUEST_COUNT * MAXB)


def shuffle_requests(sub_key):
    return jax.random.permutation(sub_key, REQUEST_COUNT)


def shuffle_adapters(sub_key):
    return jax.random.permutation(sub_key, ADAPTER_COUNT)


def layout(key):
    base_key = jax.random.fold_in(key, 101)
    sub_keys = jax.random.split(base_key, 8)
    context_output = MAXB * BLOCK_TOKENS
    replica_ids = jnp.arange(N_REPLICA, dtype=jnp.int32)
    request_ids = jnp.arange(REQUEST_COUNT, dtype=jnp.int32)
    ceiling = jax.random.randint(sub_keys[0], (N_REPLICA, 1), context_output // 4, context_output)
    raw_lengths = jax.random.randint(sub_keys[1], (N_REPLICA, REQUEST_COUNT), 0, context_output)
    length_grid = 1 + raw_lengths % ceiling
    hot_replica = jax.random.randint(sub_keys[2], (), 0, N_REPLICA)
    hot_request = jax.random.randint(sub_keys[3], (N_REPLICA,), 0, REQUEST_COUNT)
    longest = (replica_ids[:, None] == hot_replica) & (request_ids[None, :] == hot_request[:, None])
    length_grid = jnp.where(longest, context_output - 1, length_grid).astype(jnp.int32)
    tables = jax.vmap(shuffle_blocks)(jax.random.split(sub_keys[4], N_REPLICA))
    leaving = jax.vmap(shuffle_requests)(jax.random.split(sub_keys[5], N_REPLICA))[:, :MOVING_REQUESTS]
    ids_grid = jax.random.randint(sub_keys[6], (N_REPLICA, REQUEST_COUNT), 0, ADAPTER_COUNT)
    cover = jax.vmap(shuffle_adapters)(jax.random.split(sub_keys[7], N_REPLICA))
    spread = cover[:, jnp.arange(MOVING_REQUESTS) % ADAPTER_COUNT]
    ids_grid = ids_grid.at[replica_ids[:, None], leaving].set(spread)
    return (length_grid.reshape(-1).astype(jnp.int32), tables.reshape(-1, MAXB).astype(jnp.int32), leaving.reshape(-1).astype(jnp.int32), ids_grid.reshape(-1).astype(jnp.int32))


def fresh_keys(key):
    array_shape = (N_REPLICA * REQUEST_COUNT, KEY_VALUE_HEADS * HEAD_WIDTH)
    first_keys = jax.random.truncated_normal(jax.random.fold_in(key, 202), -4.0, 4.0, array_shape)
    second_keys = jax.random.truncated_normal(jax.random.fold_in(key, 203), -4.0, 4.0, array_shape)
    return (first_keys, second_keys)


def draw_first_key_value(key, part):
    own_key = jax.random.fold_in(key, 3)
    first_keys, second_keys = fresh_keys(key)
    values = jax.random.truncated_normal(own_key, -4.0, 4.0, first_keys.shape)
    return jnp.stack([first_keys, values], axis=1).astype(jnp.bfloat16)


def draw_second_key_value(key, part):
    own_key = jax.random.fold_in(key, 4)
    first_keys, second_keys = fresh_keys(key)
    values = jax.random.truncated_normal(own_key, -4.0, 4.0, second_keys.shape)
    return jnp.stack([second_keys, values], axis=1).astype(jnp.bfloat16)


def draw_first_queries(key, part):
    own_key = jax.random.fold_in(key, 5)
    array_shape = (N_REPLICA * REQUEST_COUNT, QUERY_HEADS * HEAD_WIDTH)
    queries = jax.random.truncated_normal(own_key, -4.0, 4.0, array_shape)
    return queries.astype(jnp.bfloat16)


def draw_second_queries(key, part):
    own_key = jax.random.fold_in(key, 6)
    array_shape = (N_REPLICA * REQUEST_COUNT, QUERY_HEADS * HEAD_WIDTH)
    queries = jax.random.truncated_normal(own_key, -4.0, 4.0, array_shape)
    return queries.astype(jnp.bfloat16)


def draw_key_value_pool(key, part):
    own_key = jax.random.fold_in(key, 7)
    array_shape = (N_REPLICA * BLOCK_COUNT, BLOCK_TOKENS, 2, KEY_VALUE_HEADS * HEAD_WIDTH)
    pool = jax.random.truncated_normal(own_key, -4.0, 4.0, array_shape)
    return pool.astype(jnp.bfloat16)


def draw_request_blocks(key, part):
    return layout(key)[1]


def draw_lengths(key, part):
    return layout(key)[0]


def draw_moving_request_list(key, part):
    return layout(key)[2]


def draw_adapter_index(key, part):
    return layout(key)[3]


def plant(values, key, low, high):
    spot = [jax.random.randint(jax.random.fold_in(key, axis), (), 0, length) for axis, length in enumerate(values.shape)]
    widest = values.shape.index(max(values.shape))
    next_to = spot[:widest] + [(spot[widest] + 1) % values.shape[widest]] + spot[widest + 1:]
    return values.at[tuple(spot)].set(low).at[tuple(next_to)].set(high)


def spiked(values, stream_key, source, target, shards_of, factor):
    owner, partner = [(jnp.arange(values.shape[dim]) // (values.shape[dim] // shards_of)).reshape([-1 if axis == dim else 1 for axis in range(values.ndim)]) for dim in (source, target)]
    chosen = jax.random.permutation(stream_key, shards_of)[partner]
    strong = (owner == chosen) | (owner == (partner + shards_of // 2) % shards_of)
    return jnp.where(strong, factor * values, values)


def level_of(key, dims, pieces, smallest, high):
    def one(dim, shards_of):
        steps = jax.random.uniform(jax.random.fold_in(jax.random.fold_in(key, 6), dim), (shards_of,), jnp.float32, smallest / len(pieces), high / len(pieces))
        return jnp.repeat(jnp.exp(steps), dims[dim] // shards_of).reshape((-1,) + (1,) * (len(dims) - dim - 1))

    gain = one(*pieces[0])
    for cut in pieces[1:]:
        gain = gain * one(*cut)
    return gain


def gaussian(key, dims, scale, reach, shards=(), held_as=jnp.bfloat16):
    values = scale * jax.random.normal(key, dims, jnp.float32)
    if shards:
        values = values * level_of(key, dims, shards, -0.22, 0.18)
    return jnp.clip(values, -reach, reach).astype(held_as)


def noise_with(stream_key, shape, width, bound, cuts, heavy, kind=jnp.bfloat16):
    values = width * jax.random.normal(stream_key, shape, jnp.float32)
    if cuts:
        values = values * level_of(stream_key, shape, cuts, -0.22, 0.18)
    return jnp.clip(spiked(values, jax.random.fold_in(stream_key, 3), *heavy), -bound, bound).astype(kind)


def setup_inputs(seed: int = 0) -> dict:
    keys = jax.random.split(jax.random.key(seed), 15)
    first_queries = draw_first_queries(jax.random.fold_in(keys[14], 71), 0)
    first_key_value = draw_first_key_value(jax.random.fold_in(keys[14], 71), 0)
    second_queries = draw_second_queries(jax.random.fold_in(keys[14], 71), 0)
    second_key_value = draw_second_key_value(jax.random.fold_in(keys[14], 71), 0)
    key_value_pool = draw_key_value_pool(jax.random.fold_in(keys[14], 71), 0)
    request_blocks = draw_request_blocks(jax.random.fold_in(keys[14], 71), 0)
    lengths = draw_lengths(jax.random.fold_in(keys[14], 71), 0)
    moving_request_list = draw_moving_request_list(jax.random.fold_in(keys[14], 71), 0)
    adapter_index = draw_adapter_index(jax.random.fold_in(keys[14], 71), 0)
    adapter_rank_bucket = plant(jax.random.randint(keys[9], (N_REPLICA * ADAPTER_COUNT,), 0, 4), jax.random.fold_in(keys[9], 1), 0, 3).astype(jnp.int32)
    replica_pair_mask = jax.random.randint(keys[10], (1,), 1, N_REPLICA).astype(jnp.int32)
    adapter_down_factors = gaussian(keys[11], (N_REPLICA * ADAPTER_COUNT, QUERY_HEADS * HEAD_WIDTH, PADDED_RANK), (QUERY_HEADS * HEAD_WIDTH // 16) ** -0.5, 0.25, ((0, 16), (1, 8)))
    adapter_up_factors = gaussian(keys[12], (N_REPLICA * ADAPTER_COUNT, PADDED_RANK, MODEL_WIDTH), PADDED_RANK ** -0.5, 0.5, ((0, 16), (2, 8)))
    output_weight = noise_with(keys[13], (QUERY_HEADS * HEAD_WIDTH, MODEL_WIDTH), (QUERY_HEADS * HEAD_WIDTH // 16) ** -0.5, 0.375, ((0, 8),), (0, 1, 8, 2.0))
    return {"first_queries": first_queries, "first_key_value": first_key_value, "second_queries": second_queries, "second_key_value": second_key_value, "key_value_pool": key_value_pool, "request_blocks": request_blocks, "lengths": lengths, "moving_request_list": moving_request_list, "adapter_index": adapter_index, "adapter_rank_bucket": adapter_rank_bucket, "replica_pair_mask": replica_pair_mask, "adapter_down_factors": adapter_down_factors, "adapter_up_factors": adapter_up_factors, "output_weight": output_weight}


def padding_factors(down_part, up_part, bucket_part):
    doubling_level = jnp.left_shift(jnp.ones_like(bucket_part), bucket_part)
    live_rank = (PADDED_RANK // 8) * doubling_level
    adapter_scale = 2.0 / doubling_level.astype(jnp.float32)
    visible_mask = jnp.arange(PADDED_RANK, dtype=jnp.int32)[None, :] < live_rank[:, None]
    padded_down = jnp.where(visible_mask[:, None, :], down_part, jnp.zeros_like(down_part))
    factor_matrix = jnp.where(visible_mask, adapter_scale[:, None], jnp.zeros_like(adapter_scale)[:, None])
    padded_up = (up_part.astype(jnp.float32) * factor_matrix[:, :, None]).astype(jnp.bfloat16)
    return padded_down, padded_up


def gather_blocks(pool_part, table_part, length_part):
    context_output = MAXB * BLOCK_TOKENS
    kv_cache = pool_part[table_part].reshape(table_part.shape[0], context_output, 2, pool_part.shape[-1])
    position = jnp.arange(context_output, dtype=jnp.int32)[None, :, None, None]
    return jnp.where(position < length_part[:, None, None, None], kv_cache, jnp.zeros_like(kv_cache))


def place_token(kv_cache, length_part, new_part):
    position = jnp.arange(MAXB * BLOCK_TOKENS, dtype=jnp.int32)[None, :, None, None]
    return jnp.where(position == length_part[:, None, None, None], new_part[:, None, :, :], kv_cache)


def stayers(leaving_part):
    slot_ids = jnp.arange(REQUEST_COUNT, dtype=jnp.int32)
    leaving = jnp.any(slot_ids[:, None] == leaving_part[None, :], axis=1).astype(jnp.int32)
    ranking = jnp.argsort(leaving * REQUEST_COUNT + slot_ids)
    return ranking[:REQUEST_COUNT - MOVING_REQUESTS].astype(jnp.int32)


def attend(query, kv_cache, length_part, own_new):
    row_count = query.shape[0]
    context_output = MAXB * BLOCK_TOKENS
    kv_heads = kv_cache.shape[-1] // HEAD_WIDTH
    group_size = query.shape[-1] // kv_cache.shape[-1]
    query_f = query.reshape(row_count, kv_heads, group_size, HEAD_WIDTH).astype(jnp.float32)
    keys_f = kv_cache[:, :, 0].reshape(row_count, context_output, kv_heads, HEAD_WIDTH).astype(jnp.float32)
    values_f = kv_cache[:, :, 1].reshape(row_count, context_output, kv_heads, HEAD_WIDTH).astype(jnp.float32)
    scores = jnp.einsum("rkgd,rlkd->rkgl", query_f, keys_f) * (HEAD_WIDTH ** -0.5)
    visible_mask = jnp.arange(context_output, dtype=jnp.int32)[None, None, None, :] <= length_part[:, None, None, None]
    scores = jnp.where(visible_mask, scores, -jnp.inf)
    row_max = jnp.max(scores, axis=-1)
    if own_new is not None:
        own_keys = own_new[:, 0].reshape(row_count, kv_heads, HEAD_WIDTH).astype(jnp.float32)
        own_score = jnp.einsum("rkgd,rkd->rkg", query_f, own_keys) * (HEAD_WIDTH ** -0.5)
        row_max = jnp.maximum(row_max, own_score)
    weights = jnp.exp(scores - row_max[..., None])
    row_sum = jnp.sum(weights, axis=-1)
    if own_new is not None:
        own_weight = jnp.exp(own_score - row_max)
        row_sum = row_sum + own_weight
    weights_bf = lax.optimization_barrier((weights / row_sum[..., None]).astype(jnp.bfloat16))
    blended = jnp.einsum("rkgl,rlkd->rkgd", weights_bf.astype(jnp.float32), values_f)
    if own_new is not None:
        own_values = own_new[:, 1].reshape(row_count, kv_heads, HEAD_WIDTH).astype(jnp.float32)
        own_prob = lax.optimization_barrier((own_weight / row_sum).astype(jnp.bfloat16))
        blended = blended + own_prob.astype(jnp.float32)[..., None] * own_values[:, :, None, :]
    return blended.reshape(row_count, -1).astype(jnp.bfloat16)


def project(attended, output_weight, down_pool, up_pool, adapter_pick):
    base_part = jnp.dot(attended, output_weight, preferred_element_type=jnp.float32)
    low_rank = jnp.einsum("rq,aqk->rak", attended.astype(jnp.float32), down_pool.astype(jnp.float32))
    chosen = adapter_pick[:, None] == jnp.arange(down_pool.shape[0], dtype=jnp.int32)[None, :]
    low_rank = jnp.where(chosen[:, :, None], low_rank, jnp.zeros_like(low_rank))
    adapter_part = jnp.dot(low_rank.reshape(low_rank.shape[0], -1),
                           up_pool.astype(jnp.float32).reshape(-1, up_pool.shape[-1]),
                           precision=lax.Precision.HIGHEST)
    return (base_part + adapter_part).astype(jnp.bfloat16)


def reference(first_queries, first_key_value, second_queries, second_key_value, key_value_pool, request_blocks, lengths, moving_request_list,
              adapter_index, adapter_rank_bucket, replica_pair_mask, adapter_down_factors, adapter_up_factors, output_weight):
    context_output = MAXB * BLOCK_TOKENS
    def per_replica_rows(array_in, count):
        return array_in.reshape((N_REPLICA, count) + array_in.shape[1:])
    query_one = per_replica_rows(first_queries, REQUEST_COUNT)
    token_one = per_replica_rows(first_key_value, REQUEST_COUNT)
    query_two = per_replica_rows(second_queries, REQUEST_COUNT)
    token_two = per_replica_rows(second_key_value, REQUEST_COUNT)
    pools = per_replica_rows(key_value_pool, BLOCK_COUNT)
    tables = per_replica_rows(request_blocks, REQUEST_COUNT)
    length_all = per_replica_rows(lengths, REQUEST_COUNT)
    leaving_all = per_replica_rows(moving_request_list, MOVING_REQUESTS)
    ids_all = per_replica_rows(adapter_index, REQUEST_COUNT)
    rank_groups = per_replica_rows(adapter_rank_bucket, ADAPTER_COUNT)
    padded_down, padded_up = jax.vmap(padding_factors)(per_replica_rows(adapter_down_factors, ADAPTER_COUNT), per_replica_rows(adapter_up_factors, ADAPTER_COUNT), rank_groups)
    replica_ids = jnp.arange(N_REPLICA, dtype=jnp.int32)
    partner_lookup = jnp.bitwise_xor(replica_ids, replica_pair_mask[0])

    def first_step(replica):
        kv_cache = place_token(gather_blocks(pools[replica], tables[replica], length_all[replica]),
                               length_all[replica], token_one[replica])
        attended = attend(query_one[replica], kv_cache, length_all[replica], None)
        result = project(attended, output_weight, padded_down[replica], padded_up[replica], ids_all[replica])
        return result, kv_cache[leaving_all[replica]]

    out_first, moving_rows = lax.map(first_step, replica_ids)

    def second_step(replica):
        partner = partner_lookup[replica]
        staying = stayers(leaving_all[replica])
        kv_cache = place_token(gather_blocks(pools[replica], tables[replica], length_all[replica]),
                               length_all[replica], token_one[replica])
        second_cache = jnp.concatenate([kv_cache[staying], moving_rows[partner]], axis=0)
        second_lengths = jnp.concatenate([length_all[replica][staying],
                                          length_all[partner][leaving_all[partner]]])
        attended = attend(query_two[replica], second_cache, second_lengths, token_two[replica])
        adapter_pick = jnp.concatenate([ids_all[replica][staying],
                                        ids_all[partner][leaving_all[partner]] + ADAPTER_COUNT])
        down_all = jnp.concatenate([padded_down[replica], padded_down[partner]], axis=0)
        up_all = jnp.concatenate([padded_up[replica], padded_up[partner]], axis=0)
        return project(attended, output_weight, down_all, up_all, adapter_pick)

    out_second = lax.map(second_step, replica_ids)
    incoming_cache = moving_rows[partner_lookup].reshape(N_REPLICA * MOVING_REQUESTS, context_output, 2, KEY_VALUE_HEADS * HEAD_WIDTH)
    received_down = padded_down[partner_lookup].reshape(N_REPLICA * ADAPTER_COUNT, QUERY_HEADS * HEAD_WIDTH, PADDED_RANK)
    received_up = padded_up[partner_lookup].reshape(N_REPLICA * ADAPTER_COUNT, PADDED_RANK, MODEL_WIDTH)
    return (out_first.reshape(N_REPLICA * REQUEST_COUNT, MODEL_WIDTH), out_second.reshape(N_REPLICA * REQUEST_COUNT, MODEL_WIDTH),
            incoming_cache, received_down, received_up)
```

```python
import functools

import jax
import jax.numpy as jnp
from jax import lax
from jax.experimental import pallas as pl
from jax.experimental.pallas import tpu as pltpu
from jax.sharding import PartitionSpec as P

HEAD_WIDTH = 128
GROUP = 8
PADDED_RANK = 128
REQUEST_COUNT = 16
MOVING_REQUESTS = 2
STAYING = REQUEST_COUNT - MOVING_REQUESTS
ADAPTER_COUNT = 2
BLOCK_TOKENS = 64
BLOCK_ROWS = 2 * BLOCK_TOKENS
MAXB = 8
CACHE_ROWS = MAXB * BLOCK_ROWS
MIB = 1 << 20

ANY = pl.BlockSpec(memory_space=pl.ANY)
VMEM = pl.BlockSpec(memory_space=pltpu.VMEM)
SMEM = pl.BlockSpec(memory_space=pltpu.SMEM)


def params(mib):
    return pltpu.CompilerParams(vmem_limit_bytes=mib * MIB)


def load_tables(pairs, sems):
    copies = [
        pltpu.make_async_copy(source, target, sems.at[place])
        for place, (source, target) in enumerate(pairs)
    ]
    for copy in copies:
        copy.start()
    for copy in copies:
        copy.wait()


def own_rows(ref, replica, count):
    return ref.at[pl.ds(pl.multiple_of(replica * count, count), count)]


def prepare_kernel(
    blocks_ref,
    lengths_ref,
    moving_ref,
    buckets_ref,
    pool_ref,
    token_ref,
    query_ref,
    second_token_ref,
    down_ref,
    up_ref,
    cache_out,
    down_out,
    up_out,
    query_out,
    blocks,
    lengths,
    moving,
    buckets,
    gathered,
    table_sems,
    sems,
):
    replica = lax.axis_index("replica")
    load_tables(
        [
            (own_rows(blocks_ref, replica, REQUEST_COUNT), blocks),
            (lengths_ref, lengths),
            (moving_ref, moving),
            (buckets_ref, buckets),
        ],
        table_sems,
    )
    copies = []
    for slot in range(MOVING_REQUESTS):
        request = moving[replica * MOVING_REQUESTS + slot]
        for block in range(MAXB):
            copy = pltpu.make_async_copy(
                pool_ref.at[blocks[request, block]],
                gathered.at[slot, pl.ds(block * BLOCK_ROWS, BLOCK_ROWS)],
                sems.at[slot, block],
            )
            copy.start()
            copies.append(copy)
    for slot in range(ADAPTER_COUNT):
        bucket = buckets[replica * ADAPTER_COUNT + slot]
        level = jnp.left_shift(1, bucket)
        live = PADDED_RANK // 8 * level
        scale = 2.0 / level.astype(jnp.float32)
        lane = lax.broadcasted_iota(jnp.int32, down_ref.shape[1:], 1)
        down_part = down_ref[slot].astype(jnp.float32)
        down_out[slot] = jnp.where(lane < live, down_part, 0.0).astype(jnp.bfloat16)
        rank = lax.broadcasted_iota(jnp.int32, up_ref.shape[1:], 0)
        up_part = up_ref[slot].astype(jnp.float32) * scale
        up_out[slot] = jnp.where(rank < live, up_part, 0.0).astype(jnp.bfloat16)
    for slot in range(MOVING_REQUESTS):
        row = STAYING + slot
        heads = [
            query_ref[row : row + 1, h * HEAD_WIDTH : (h + 1) * HEAD_WIDTH].astype(jnp.float32)
            for h in range(GROUP)
        ]
        own = second_token_ref[row].astype(jnp.float32)
        rest = jnp.zeros((16 - GROUP - 2, HEAD_WIDTH), jnp.float32)
        query_out[slot] = jnp.concatenate(heads + [own, rest], axis=0).astype(jnp.bfloat16)
    for copy in copies:
        copy.wait()
    for slot in range(MOVING_REQUESTS):
        request = moving[replica * MOVING_REQUESTS + slot]
        length = lengths[replica * REQUEST_COUNT + request]
        token = token_ref[request].astype(jnp.float32)
        row = lax.broadcasted_iota(jnp.int32, (CACHE_ROWS, HEAD_WIDTH), 0)
        position = jnp.right_shift(row, 1)
        own = jnp.where(jnp.bitwise_and(row, 1) == 0, token[0:1], token[1:2])
        held = gathered[slot].astype(jnp.float32)
        kept = jnp.where(position < length, held, jnp.where(position == length, own, 0.0))
        cache_out[slot] = kept.astype(jnp.bfloat16)


def prepare(tables, pool, token, query, second_token, down, up):
    return pl.pallas_call(
        prepare_kernel,
        out_shape=(
            jax.ShapeDtypeStruct((MOVING_REQUESTS, CACHE_ROWS, HEAD_WIDTH), jnp.bfloat16),
            jax.ShapeDtypeStruct(down.shape, jnp.bfloat16),
            jax.ShapeDtypeStruct(up.shape, jnp.bfloat16),
            jax.ShapeDtypeStruct((MOVING_REQUESTS, 16, HEAD_WIDTH), jnp.bfloat16),
        ),
        in_specs=[ANY] * 5 + [VMEM] * 5,
        out_specs=(VMEM,) * 4,
        scratch_shapes=[
            pltpu.SMEM((REQUEST_COUNT, MAXB), jnp.int32),
            pltpu.SMEM(tables[1].shape, jnp.int32),
            pltpu.SMEM(tables[2].shape, jnp.int32),
            pltpu.SMEM(tables[4].shape, jnp.int32),
            pltpu.VMEM((MOVING_REQUESTS, CACHE_ROWS, HEAD_WIDTH), jnp.bfloat16),
            pltpu.SemaphoreType.DMA((4,)),
            pltpu.SemaphoreType.DMA((MOVING_REQUESTS, MAXB)),
        ],
        compiler_params=params(16),
        cost_estimate=pl.CostEstimate(flops=10**6, bytes_accessed=3 * MIB, transcendentals=0),
        name="prepare",
    )(tables[0], tables[1], tables[2], tables[4], pool, token, query, second_token, down, up)


def attend_kernel(
    blocks_ref,
    lengths_ref,
    moving_ref,
    picks_ref,
    pool_ref,
    weight_ref,
    query_ref,
    token_ref,
    second_query_ref,
    second_token_ref,
    arrived_ref,
    down_ref,
    shares_out,
    picks_out,
    blocks,
    lengths,
    moving,
    picks,
    pool,
    weight,
    queries,
    second_queries,
    tokens,
    second_tokens,
    attended,
    pick_rows,
    table_sems,
    pool_sems,
    weight_sems,
):
    replica = lax.axis_index("replica")
    parts = shares_out.shape[0]
    width = weight_ref.shape[1] // parts
    pool_parts = pool_sems.shape[0]
    per_part = pool_ref.shape[0] // pool_parts

    def pool_copy(part):
        where = pl.ds(part * per_part, per_part)
        return pltpu.make_async_copy(pool_ref.at[where], pool.at[where], pool_sems.at[part])

    def weight_copy(part):
        columns = pl.ds(pl.multiple_of(part * width, width), width)
        return pltpu.make_async_copy(
            weight_ref.at[:, columns], weight.at[part], weight_sems.at[part]
        )

    for part in range(pool_parts):
        pool_copy(part).start()
    for part in range(parts):
        weight_copy(part).start()
    load_tables(
        [
            (own_rows(blocks_ref, replica, REQUEST_COUNT), blocks),
            (lengths_ref, lengths),
            (moving_ref, moving),
            (picks_ref, picks),
        ],
        table_sems,
    )
    for h in range(GROUP):
        columns = slice(h * HEAD_WIDTH, (h + 1) * HEAD_WIDTH)
        rows = pl.ds(h, REQUEST_COUNT, stride=GROUP)
        queries[rows, :] = query_ref[:, columns].astype(jnp.float32)
        second_queries[rows, :] = second_query_ref[:, columns].astype(jnp.float32)
    tokens[:, 0:2, :] = token_ref[...].astype(jnp.float32)
    second_tokens[:, 0:2, :] = second_token_ref[...].astype(jnp.float32)
    for slot in range(MOVING_REQUESTS):
        row = STAYING + slot
        arrived = arrived_ref[slot].astype(jnp.float32)
        second_queries[row * GROUP : (row + 1) * GROUP, :] = arrived[0:GROUP]
        second_tokens[row, 0:2, :] = arrived[GROUP : GROUP + 2]
    for part in range(pool_parts):
        pool_copy(part).wait()

    leaving = [moving[replica * MOVING_REQUESTS + slot] for slot in range(MOVING_REQUESTS)]
    lane = lax.broadcasted_iota(jnp.int32, (2 * GROUP, CACHE_ROWS), 1)
    position = jnp.right_shift(lane, 1)
    is_key = jnp.bitwise_and(lane, 1) == 0
    second_half = lax.broadcasted_iota(jnp.int32, (2 * GROUP, 1), 0) >= GROUP

    def one_request(request):
        second_row = request
        for slot in range(MOVING_REQUESTS):
            second_row = second_row - (leaving[slot] < request).astype(jnp.int32)
        for slot in range(MOVING_REQUESTS):
            second_row = jnp.where(leaving[slot] == request, STAYING + slot, second_row)
        length = lengths[replica * REQUEST_COUNT + request]
        pick = picks[replica * REQUEST_COUNT + request].astype(jnp.float32)
        pick_rows[pl.ds(request, 1), :] = jnp.full((1, HEAD_WIDTH), pick, jnp.float32)
        pick_rows[pl.ds(REQUEST_COUNT + second_row, 1), :] = jnp.full(
            (1, HEAD_WIDTH), pick, jnp.float32
        )
        first_rows = pl.ds(pl.multiple_of(request * GROUP, GROUP), GROUP)
        second_rows = pl.ds(pl.multiple_of(second_row * GROUP, GROUP), GROUP)
        query = jnp.concatenate([queries[first_rows, :], second_queries[second_rows, :]], axis=0)
        held = jnp.concatenate([pool[blocks[request, b]] for b in range(MAXB)], axis=0)
        token = tokens[request]
        own = second_tokens[second_row]
        scale = HEAD_WIDTH ** (-0.5)
        scores = lax.dot_general(
            query.astype(jnp.bfloat16),
            held,
            (((1,), (1,)), ((), ())),
            preferred_element_type=jnp.float32,
        )
        scores = jnp.where(is_key & (position < length), scores * scale, -jnp.inf)
        token_score = jnp.sum(query * token[0:1], axis=1, keepdims=True) * scale
        own_score = jnp.sum(query * own[0:1], axis=1, keepdims=True) * scale
        own_score = jnp.where(second_half, own_score, -jnp.inf)
        row_max = jnp.max(scores, axis=1, keepdims=True)
        row_max = jnp.maximum(row_max, jnp.maximum(token_score, own_score))
        weights = jnp.exp(scores - row_max)
        token_weight = jnp.exp(token_score - row_max)
        own_weight = jnp.exp(own_score - row_max)
        row_sum = jnp.sum(weights, axis=1, keepdims=True) + token_weight + own_weight
        weights = pltpu.roll(weights / row_sum, 1, 1).astype(jnp.bfloat16)
        token_weight = (token_weight / row_sum).astype(jnp.bfloat16).astype(jnp.float32)
        own_weight = (own_weight / row_sum).astype(jnp.bfloat16).astype(jnp.float32)
        blended = jnp.dot(weights, held, preferred_element_type=jnp.float32)
        blended = blended + token_weight * token[1:2] + own_weight * own[1:2]
        attended[first_rows, :] = blended[0:GROUP]
        attended[
            pl.ds(pl.multiple_of((REQUEST_COUNT + second_row) * GROUP, GROUP), GROUP), :
        ] = blended[GROUP : 2 * GROUP]

    unrolled = 4

    def some_requests(step, carry):
        for k in range(unrolled):
            one_request(step * unrolled + k)
        return carry

    lax.fori_loop(0, REQUEST_COUNT // unrolled, some_requests, 0)

    rows = 2 * REQUEST_COUNT
    held = jnp.concatenate(
        [attended[pl.ds(h, rows, stride=GROUP), :] for h in range(GROUP)], axis=1
    ).astype(jnp.bfloat16)
    pick_all = pick_rows[...]
    picks_out[...] = pick_all
    low = jnp.zeros((rows, PADDED_RANK), jnp.float32)
    for slot in range(ADAPTER_COUNT):
        part = jnp.dot(held, down_ref[slot], preferred_element_type=jnp.float32)
        low = jnp.where(pick_all == slot, part, low)
    low = low.astype(jnp.bfloat16)

    def one_part(part, carry):
        weight_copy(part).wait()
        share = jnp.dot(held, weight[part], preferred_element_type=jnp.float32)
        shares_out[part, :, 0:width] = share.astype(jnp.bfloat16)
        shares_out[part, :, width:] = low
        return carry

    lax.fori_loop(0, parts, one_part, 0)


def attend(tables, pool, weight, query, token, second_query, second_token, arrived, down, parts):
    rows = 2 * REQUEST_COUNT
    width = weight.shape[1] // parts
    depth = weight.shape[0]
    return pl.pallas_call(
        attend_kernel,
        out_shape=(
            jax.ShapeDtypeStruct((parts, rows, width + PADDED_RANK), jnp.bfloat16),
            jax.ShapeDtypeStruct((rows, PADDED_RANK), jnp.float32),
        ),
        in_specs=[ANY] * 6 + [VMEM] * 6,
        out_specs=(VMEM,) * 2,
        scratch_shapes=[
            pltpu.SMEM((REQUEST_COUNT, MAXB), jnp.int32),
            pltpu.SMEM(tables[1].shape, jnp.int32),
            pltpu.SMEM(tables[2].shape, jnp.int32),
            pltpu.SMEM(tables[3].shape, jnp.int32),
            pltpu.VMEM(pool.shape, jnp.bfloat16),
            pltpu.VMEM((parts, depth, width), jnp.bfloat16),
            pltpu.VMEM((REQUEST_COUNT * GROUP, HEAD_WIDTH), jnp.float32),
            pltpu.VMEM((REQUEST_COUNT * GROUP, HEAD_WIDTH), jnp.float32),
            pltpu.VMEM((REQUEST_COUNT, 8, HEAD_WIDTH), jnp.float32),
            pltpu.VMEM((REQUEST_COUNT, 8, HEAD_WIDTH), jnp.float32),
            pltpu.VMEM((rows * GROUP, HEAD_WIDTH), jnp.float32),
            pltpu.VMEM((rows, HEAD_WIDTH), jnp.float32),
            pltpu.SemaphoreType.DMA((4,)),
            pltpu.SemaphoreType.DMA((4,)),
            pltpu.SemaphoreType.DMA((parts,)),
        ],
        compiler_params=params(40),
        cost_estimate=pl.CostEstimate(
            flops=2 * rows * depth * weight.shape[1], bytes_accessed=21 * MIB, transcendentals=10**5
        ),
        name="attend_project",
    )(
        tables[0],
        tables[1],
        tables[2],
        tables[3],
        pool,
        weight,
        query,
        token,
        second_query,
        second_token,
        arrived,
        down,
    )


def finish_kernel(shares_ref, picks_ref, up_ref, first_out, second_out, leaving_out):
    parts, rows, _ = shares_ref.shape
    width = first_out.shape[1]
    total = shares_ref[0].astype(jnp.float32)
    for part in range(1, parts):
        total = total + shares_ref[part].astype(jnp.float32)
    base, low = total[:, 0:width], total[:, width:]
    picks = picks_ref[...]
    for slot in range(ADAPTER_COUNT):
        rest = jnp.where(picks == slot, low, 0.0)
        pieces = []
        for _ in range(3):
            piece = rest.astype(jnp.bfloat16)
            rest = rest - piece.astype(jnp.float32)
            pieces.append(piece)
        stacked = jnp.concatenate(pieces, axis=0)
        part = jnp.dot(stacked, up_ref[slot], preferred_element_type=jnp.float32)
        base = base + (part[0:rows] + part[rows : 2 * rows] + part[2 * rows : 3 * rows])
    result = base.astype(jnp.bfloat16)
    first_out[...] = result[0:REQUEST_COUNT]
    second_out[...] = result[REQUEST_COUNT:]
    leaving_out[...] = base[REQUEST_COUNT + STAYING :].astype(jnp.bfloat16)


def finish(shares, picks, up):
    width = shares.shape[2] - PADDED_RANK
    return pl.pallas_call(
        finish_kernel,
        out_shape=(
            jax.ShapeDtypeStruct((REQUEST_COUNT, width), jnp.bfloat16),
            jax.ShapeDtypeStruct((REQUEST_COUNT, width), jnp.bfloat16),
            jax.ShapeDtypeStruct((MOVING_REQUESTS, width), jnp.bfloat16),
        ),
        in_specs=[VMEM] * 3,
        out_specs=(VMEM,) * 3,
        compiler_params=params(16),
        cost_estimate=pl.CostEstimate(flops=5 * 10**7, bytes_accessed=MIB, transcendentals=0),
        name="finish",
    )(shares, picks, up)


def branch(mask, tables, pool, weight, arrays, sent):
    query, token, second_query, second_token = arrays
    cache, down, up, moved_query = sent
    count = lax.axis_size("replica")
    pairs = [(source, source ^ mask) for source in range(count)]
    swap = functools.partial(lax.ppermute, axis_name="replica", perm=pairs)
    arrived = swap(moved_query)
    got_cache, got_down, got_up = swap(cache), swap(down), swap(up)
    shares, picks = attend(
        tables,
        pool,
        weight,
        query,
        token,
        second_query,
        second_token,
        arrived,
        down,
        lax.axis_size("tensor"),
    )
    shares = lax.all_to_all(shares, "tensor", 0, 0, tiled=True)
    first, second, leaving = finish(shares, picks, up)
    second = lax.dynamic_update_slice(second, swap(leaving), (STAYING, 0))
    return first, second, got_cache, got_down, got_up


def shards(
    first_queries,
    first_key_value,
    second_queries,
    second_key_value,
    key_value_pool,
    request_blocks,
    lengths,
    moving_request_list,
    adapter_index,
    adapter_rank_bucket,
    replica_pair_mask,
    adapter_down_factors,
    adapter_up_factors,
    output_weight,
):
    tables = (request_blocks, lengths, moving_request_list, adapter_index, adapter_rank_bucket)
    pool = key_value_pool.reshape(key_value_pool.shape[0], BLOCK_ROWS, HEAD_WIDTH)
    sent = prepare(
        tables,
        pool,
        first_key_value,
        second_queries,
        second_key_value,
        adapter_down_factors,
        adapter_up_factors,
    )
    arrays = (first_queries, first_key_value, second_queries, second_key_value)
    branches = [
        functools.partial(branch, mask) for mask in range(1, lax.axis_size("replica"))
    ]
    first, second, cache, down, up = lax.switch(
        replica_pair_mask[0] - 1, branches, tables, pool, output_weight, arrays, sent
    )
    cache = cache.reshape(MOVING_REQUESTS, MAXB * BLOCK_TOKENS, 2, HEAD_WIDTH)
    return first, second, cache, down, up


def solution(mesh):
    placed = (
        P("replica", "tensor"),
        P("replica", None, "tensor"),
        P("replica", "tensor"),
        P("replica", None, "tensor"),
        P("replica", None, None, "tensor"),
        P(),
        P(),
        P(),
        P(),
        P(),
        P(),
        P("replica", "tensor", None),
        P("replica", None, "tensor"),
        P("tensor", None),
    )
    return jax.shard_map(
        shards,
        mesh=mesh,
        in_specs=placed,
        out_specs=(
            P("replica", "tensor"),
            P("replica", "tensor"),
            P("replica", None, None, "tensor"),
            P("replica", "tensor", None),
            P("replica", None, "tensor"),
        ),
        check_vma=False,
    )
```

```python
import functools

import jax
import jax.numpy as jnp
from jax import lax
from jax.experimental import pallas as pl
from jax.experimental.pallas import tpu as pltpu
from jax.sharding import PartitionSpec as P

HEAD_WIDTH = 128
GROUP = 8
PADDED_RANK = 128
REQUEST_COUNT = 16
MOVING_REQUESTS = 2
STAYING = REQUEST_COUNT - MOVING_REQUESTS
ADAPTER_COUNT = 2
BLOCK_TOKENS = 64
BLOCK_ROWS = 2 * BLOCK_TOKENS
MAXB = 8
CACHE_ROWS = MAXB * BLOCK_ROWS
MIB = 1 << 20

UNIT_ROWS = 128
RANK_UNIT = 16
ADAPTER_UNITS = PADDED_RANK // RANK_UNIT
MOST_UNITS = MOVING_REQUESTS * MAXB + 2 * ADAPTER_COUNT * ADAPTER_UNITS

ANY = pl.BlockSpec(memory_space=pl.ANY)
VMEM = pl.BlockSpec(memory_space=pltpu.VMEM)
SMEM = pl.BlockSpec(memory_space=pltpu.SMEM)


def params(mib):
    return pltpu.CompilerParams(vmem_limit_bytes=mib * MIB)


def cost(flops, moved):
    return pl.CostEstimate(flops=flops, bytes_accessed=moved, transcendentals=0)


def copies_of(pairs, sems):
    return [
        pltpu.make_async_copy(source, target, sems.at[place])
        for place, (source, target) in enumerate(pairs)
    ]


def start_all(copies):
    for copy in copies:
        copy.start()


def wait_all(copies):
    for copy in copies:
        copy.wait()


def unit_layout(replica, lengths, moving, buckets):
    counts = []
    for slot in range(MOVING_REQUESTS):
        request = moving[replica * MOVING_REQUESTS + slot]
        length = lengths[replica * REQUEST_COUNT + request]
        counts.append(lax.div(length, BLOCK_TOKENS) + 1)
    levels = [
        jnp.left_shift(jnp.int32(1), buckets[replica * ADAPTER_COUNT + slot])
        for slot in range(ADAPTER_COUNT)
    ]
    counts = counts + levels + levels
    starts, total = [], jnp.int32(0)
    for count in counts:
        starts.append(total)
        total = total + count
    return counts, starts, total


def pack_down(source, bucket):
    rows = UNIT_ROWS << bucket
    lanes = RANK_UNIT << bucket
    lane = lax.broadcasted_iota(jnp.int32, (rows, PADDED_RANK), 1)
    packed = jnp.zeros((rows, PADDED_RANK), jnp.float32)
    for group in range(PADDED_RANK // lanes):
        part = source[group * rows : (group + 1) * rows, :].astype(jnp.float32)
        if group:
            part = pltpu.roll(part, group * lanes, 1)
        here = (lane >= group * lanes) & (lane < (group + 1) * lanes)
        packed = jnp.where(here, part, packed)
    return packed.astype(jnp.bfloat16)


def prepare_kernel(
    lengths_ref,
    moving_ref,
    buckets_ref,
    mask_ref,
    blocks_ref,
    pool_ref,
    token_ref,
    query_ref,
    second_token_ref,
    down_ref,
    up_ref,
    choice_out,
    query_out,
    units,
    lengths,
    moving,
    buckets,
    mask,
    blocks,
    tokens,
    queries,
    second_tokens,
    down,
    up,
    table_sems,
    sems,
    block_sems,
):
    replica = lax.axis_index("replica")
    tables = copies_of(
        [
            (lengths_ref, lengths),
            (moving_ref, moving),
            (buckets_ref, buckets),
            (mask_ref, mask),
            (blocks_ref, blocks),
        ],
        table_sems,
    )
    arrays = copies_of(
        [
            (query_ref, queries),
            (second_token_ref, second_tokens),
            (token_ref, tokens),
            (down_ref, down),
            (up_ref, up),
        ],
        sems,
    )
    start_all(tables)
    start_all(arrays)
    wait_all(tables)
    counts, starts, _ = unit_layout(replica, lengths, moving, buckets)
    requests = [moving[replica * MOVING_REQUESTS + slot] for slot in range(MOVING_REQUESTS)]

    def block_copy(slot, block):
        return pltpu.make_async_copy(
            pool_ref.at[blocks[block, replica * REQUEST_COUNT + requests[slot]]],
            units.at[starts[slot] + block],
            block_sems.at[slot, block],
        )

    for slot in range(MOVING_REQUESTS):
        for block in range(MAXB):
            pl.when(block < counts[slot])(lambda s=slot, b=block: block_copy(s, b).start())

    choice_out[0] = jnp.right_shift(mask[0], 1)
    choice_out[1] = jnp.bitwise_and(mask[0], 1)

    wait_all(arrays[:3])
    for slot in range(MOVING_REQUESTS):
        row = STAYING + slot
        heads = [
            queries[row : row + 1, h * HEAD_WIDTH : (h + 1) * HEAD_WIDTH].astype(jnp.float32)
            for h in range(GROUP)
        ]
        own = second_tokens[row].astype(jnp.float32)
        padding = jnp.zeros((16 - GROUP - 2, HEAD_WIDTH), jnp.float32)
        query_out[slot] = jnp.concatenate(heads + [own, padding], axis=0).astype(jnp.bfloat16)
    wait_all(arrays[3:])
    for slot in range(ADAPTER_COUNT):
        bucket = buckets[replica * ADAPTER_COUNT + slot]
        level = jnp.left_shift(jnp.int32(1), bucket)
        scale = 2.0 / level.astype(jnp.float32)
        base = starts[MOVING_REQUESTS + slot]
        for kind in range(4):

            @pl.when(bucket == kind)
            def _(kind=kind, slot=slot, base=base):
                packed = pack_down(down.at[slot], kind)
                for unit in range(1 << kind):
                    units[base + unit] = packed[unit * UNIT_ROWS : (unit + 1) * UNIT_ROWS]

        base = starts[MOVING_REQUESTS + ADAPTER_COUNT + slot]

        def up_unit(unit, carry, slot=slot, base=base, scale=scale):
            ranks = pl.ds(pl.multiple_of(unit * RANK_UNIT, RANK_UNIT), RANK_UNIT)
            part = (up[slot, ranks, :].astype(jnp.float32) * scale).astype(jnp.bfloat16)
            for column in range(UNIT_ROWS // RANK_UNIT):
                units[base + unit, column * RANK_UNIT : (column + 1) * RANK_UNIT, :] = part[
                    :, column * HEAD_WIDTH : (column + 1) * HEAD_WIDTH
                ]
            return carry

        lax.fori_loop(0, level, up_unit, 0)
    for slot in range(MOVING_REQUESTS):
        for block in range(MAXB):
            pl.when(block < counts[slot])(lambda s=slot, b=block: block_copy(s, b).wait())
        length = lengths[replica * REQUEST_COUNT + requests[slot]]
        token = tokens[requests[slot]].astype(jnp.float32)
        row = lax.broadcasted_iota(jnp.int32, (UNIT_ROWS, HEAD_WIDTH), 0)
        position = jnp.right_shift(row, 1) + (counts[slot] - 1) * BLOCK_TOKENS
        own = jnp.where(jnp.bitwise_and(row, 1) == 0, token[0:1], token[1:2])
        last = starts[slot] + counts[slot] - 1
        held = units[last].astype(jnp.float32)
        kept = jnp.where(position < length, held, jnp.where(position == length, own, 0.0))
        units[last] = kept.astype(jnp.bfloat16)


def prepare(tables, mask, pool, token, query, second_token, down, up):
    blocks, lengths, moving, _, buckets = tables
    return pl.pallas_call(
        prepare_kernel,
        out_shape=(
            jax.ShapeDtypeStruct((2,), jnp.int32),
            jax.ShapeDtypeStruct((MOVING_REQUESTS, 16, HEAD_WIDTH), jnp.bfloat16),
            jax.ShapeDtypeStruct((MOST_UNITS, UNIT_ROWS, HEAD_WIDTH), jnp.bfloat16),
        ),
        in_specs=[ANY] * 11,
        out_specs=(SMEM, VMEM, VMEM),
        scratch_shapes=[
            pltpu.SMEM(lengths.shape, jnp.int32),
            pltpu.SMEM(moving.shape, jnp.int32),
            pltpu.SMEM(buckets.shape, jnp.int32),
            pltpu.SMEM(mask.shape, jnp.int32),
            pltpu.SMEM(blocks.shape, jnp.int32),
            pltpu.VMEM(token.shape, jnp.bfloat16),
            pltpu.VMEM(query.shape, jnp.bfloat16),
            pltpu.VMEM(second_token.shape, jnp.bfloat16),
            pltpu.VMEM(down.shape, jnp.bfloat16),
            pltpu.VMEM(up.shape, jnp.bfloat16),
            pltpu.SemaphoreType.DMA((5,)),
            pltpu.SemaphoreType.DMA((5,)),
            pltpu.SemaphoreType.DMA((MOVING_REQUESTS, MAXB)),
        ],
        compiler_params=params(16),
        cost_estimate=cost(10**6, 3 * MIB),
        name="prepare",
    )(lengths, moving, buckets, mask, blocks, pool, token, query, second_token, down, up)


def unpack_kernel(
    lengths_ref,
    moving_ref,
    buckets_ref,
    mask_ref,
    units,
    second_ref,
    rows_ref,
    second_out,
    cache_out,
    down_out,
    up_out,
    lengths,
    moving,
    buckets,
    mask,
    zeros,
    down,
    up,
    table_sems,
    block_sems,
    out_sems,
):
    tables = copies_of(
        [
            (lengths_ref, lengths),
            (moving_ref, moving),
            (buckets_ref, buckets),
            (mask_ref, mask),
        ],
        table_sems,
    )
    start_all(tables)
    zeros[...] = jnp.zeros_like(zeros)
    kept = second_ref[0:STAYING, :].astype(jnp.float32)
    came = rows_ref[...].astype(jnp.float32)
    second_out[...] = jnp.concatenate([kept, came], axis=0).astype(jnp.bfloat16)
    wait_all(tables)
    mate = jnp.bitwise_xor(lax.axis_index("replica"), mask[0])
    counts, starts, _ = unit_layout(mate, lengths, moving, buckets)

    def block_copy(slot, block, source):
        return pltpu.make_async_copy(
            source,
            cache_out.at[slot, pl.ds(block * BLOCK_ROWS, BLOCK_ROWS)],
            block_sems.at[slot, block],
        )

    for slot in range(MOVING_REQUESTS):
        for block in range(MAXB):
            pl.when(block < counts[slot])(
                lambda s=slot, b=block: block_copy(s, b, units.at[starts[s] + b]).start()
            )
            pl.when(block >= counts[slot])(lambda s=slot, b=block: block_copy(s, b, zeros).start())
    outs = []
    for slot in range(ADAPTER_COUNT):
        bucket = buckets[mate * ADAPTER_COUNT + slot]
        base = starts[MOVING_REQUESTS + slot]
        for kind in range(4):

            @pl.when(bucket == kind)
            def _(kind=kind, slot=slot, base=base):
                rows = UNIT_ROWS << kind
                lanes = RANK_UNIT << kind
                packed = jnp.concatenate(
                    [units[base + unit] for unit in range(1 << kind)], axis=0
                ).astype(jnp.float32)
                lane = lax.broadcasted_iota(jnp.int32, packed.shape, 1)
                for group in range(PADDED_RANK // lanes):
                    part = packed
                    if group:
                        part = pltpu.roll(part, PADDED_RANK - group * lanes, 1)
                    part = jnp.where(lane < lanes, part, 0.0).astype(jnp.bfloat16)
                    down[slot, group * rows : (group + 1) * rows, :] = part

        outs.append(pltpu.make_async_copy(down.at[slot], down_out.at[slot], out_sems.at[0, slot]))
        outs[-1].start()
        level = counts[MOVING_REQUESTS + slot]
        base = starts[MOVING_REQUESTS + ADAPTER_COUNT + slot]

        def up_unit(unit, carry, slot=slot, base=base, level=level):
            ranks = pl.ds(pl.multiple_of(unit * RANK_UNIT, RANK_UNIT), RANK_UNIT)
            held = units[base + jnp.minimum(unit, level - 1)]
            for column in range(UNIT_ROWS // RANK_UNIT):
                part = held[column * RANK_UNIT : (column + 1) * RANK_UNIT]
                up[slot, ranks, column * HEAD_WIDTH : (column + 1) * HEAD_WIDTH] = jnp.where(
                    unit < level, part, jnp.zeros_like(part)
                )
            return carry

        lax.fori_loop(0, ADAPTER_UNITS, up_unit, 0)
        outs.append(pltpu.make_async_copy(up.at[slot], up_out.at[slot], out_sems.at[1, slot]))
        outs[-1].start()
    for slot in range(MOVING_REQUESTS):
        for block in range(MAXB):
            block_copy(slot, block, zeros).wait()
    wait_all(outs)


def unpack(tables, mask, units, second, rows, down, up):
    _, lengths, moving, _, buckets = tables
    return pl.pallas_call(
        unpack_kernel,
        out_shape=(
            jax.ShapeDtypeStruct(second.shape, jnp.bfloat16),
            jax.ShapeDtypeStruct((MOVING_REQUESTS, CACHE_ROWS, HEAD_WIDTH), jnp.bfloat16),
            jax.ShapeDtypeStruct(down.shape, jnp.bfloat16),
            jax.ShapeDtypeStruct(up.shape, jnp.bfloat16),
        ),
        in_specs=[ANY] * 4 + [VMEM] * 3,
        out_specs=(VMEM,) + (ANY,) * 3,
        scratch_shapes=[
            pltpu.SMEM(lengths.shape, jnp.int32),
            pltpu.SMEM(moving.shape, jnp.int32),
            pltpu.SMEM(buckets.shape, jnp.int32),
            pltpu.SMEM(mask.shape, jnp.int32),
            pltpu.VMEM((BLOCK_ROWS, HEAD_WIDTH), jnp.bfloat16),
            pltpu.VMEM(down.shape, jnp.bfloat16),
            pltpu.VMEM(up.shape, jnp.bfloat16),
            pltpu.SemaphoreType.DMA((4,)),
            pltpu.SemaphoreType.DMA((MOVING_REQUESTS, MAXB)),
            pltpu.SemaphoreType.DMA((2, ADAPTER_COUNT)),
        ],
        compiler_params=params(16),
        cost_estimate=cost(10**6, 3 * MIB),
        name="unpack",
    )(lengths, moving, buckets, mask, units, second, rows)


def attend_kernel(
    arrived_ref,
    lengths_ref,
    moving_ref,
    buckets_ref,
    picks_ref,
    blocks_ref,
    pool_ref,
    query_ref,
    token_ref,
    second_query_ref,
    second_token_ref,
    down_ref,
    up_ref,
    weight_ref,
    shares_out,
    picks_out,
    up_out,
    lengths,
    moving,
    buckets,
    picks,
    blocks,
    raw_query,
    raw_token,
    raw_second_query,
    raw_second_token,
    down,
    pool,
    weight,
    queries,
    second_queries,
    tokens,
    second_tokens,
    attended,
    scores,
    pick_rows,
    table_sems,
    sems,
    pool_sems,
    weight_sems,
):
    replica = lax.axis_index("replica")
    parts = shares_out.shape[0]
    width = weight_ref.shape[1] // parts
    pool_parts = pool_sems.shape[0]
    per_part = pool_ref.shape[0] // pool_parts

    def pool_copy(part):
        where = pl.ds(part * per_part, per_part)
        return pltpu.make_async_copy(pool_ref.at[where], pool.at[where], pool_sems.at[part])

    def weight_copy(part):
        columns = pl.ds(pl.multiple_of(part * width, width), width)
        return pltpu.make_async_copy(
            weight_ref.at[:, columns], weight.at[part], weight_sems.at[part]
        )

    tables = copies_of(
        [
            (lengths_ref, lengths),
            (moving_ref, moving),
            (buckets_ref, buckets),
            (picks_ref, picks),
            (blocks_ref, blocks),
        ],
        table_sems,
    )
    arrays = copies_of(
        [
            (query_ref, raw_query),
            (token_ref, raw_token),
            (second_query_ref, raw_second_query),
            (second_token_ref, raw_second_token),
            (down_ref, down),
            (up_ref, up_out),
        ],
        sems,
    )
    start_all(tables)
    start_all(arrays[:4])
    for part in range(pool_parts):
        pool_copy(part).start()
    wait_all(arrays[:4])
    for h in range(GROUP):
        columns = slice(h * HEAD_WIDTH, (h + 1) * HEAD_WIDTH)
        rows = pl.ds(h, REQUEST_COUNT, stride=GROUP)
        queries[rows, :] = raw_query[:, columns].astype(jnp.float32)
        second_queries[rows, :] = raw_second_query[:, columns].astype(jnp.float32)
    tokens[:, 0:2, :] = raw_token[...].astype(jnp.float32)
    second_tokens[:, 0:2, :] = raw_second_token[...].astype(jnp.float32)
    for slot in range(MOVING_REQUESTS):
        row = STAYING + slot
        arrived = arrived_ref[slot].astype(jnp.float32)
        second_queries[row * GROUP : (row + 1) * GROUP, :] = arrived[0:GROUP]
        second_tokens[row, 0:2, :] = arrived[GROUP : GROUP + 2]
    wait_all(tables)
    for part in range(pool_parts):
        pool_copy(part).wait()
    for part in range(parts):
        weight_copy(part).start()
    start_all(arrays[4:])

    leaving = [moving[replica * MOVING_REQUESTS + slot] for slot in range(MOVING_REQUESTS)]
    lane = lax.broadcasted_iota(jnp.int32, (2 * GROUP, CACHE_ROWS), 1)
    position = jnp.right_shift(lane, 1)
    is_key = jnp.bitwise_and(lane, 1) == 0
    second_half = lax.broadcasted_iota(jnp.int32, (2 * GROUP, 1), 0) >= GROUP

    scale = HEAD_WIDTH ** (-0.5)

    def second_row_of(request):
        second_row = request
        for slot in range(MOVING_REQUESTS):
            second_row = second_row - (leaving[slot] < request).astype(jnp.int32)
        for slot in range(MOVING_REQUESTS):
            second_row = jnp.where(leaving[slot] == request, STAYING + slot, second_row)
        return second_row

    def rows_of(row):
        return pl.ds(pl.multiple_of(row * GROUP, GROUP), GROUP)

    def held_of(request):
        return jnp.concatenate([pool[blocks[b, replica * REQUEST_COUNT + request]] for b in range(MAXB)], axis=0)

    def score_request(request):
        second_row = second_row_of(request)
        query = jnp.concatenate(
            [queries[rows_of(request), :], second_queries[rows_of(second_row), :]], axis=0
        )
        length = lengths[replica * REQUEST_COUNT + request]
        dots = lax.dot_general(
            query.astype(jnp.bfloat16),
            held_of(request),
            (((1,), (1,)), ((), ())),
            preferred_element_type=jnp.float32,
        )
        scores[request] = jnp.where(is_key & (position < length), dots * scale, -jnp.inf)

    def blend_request(request):
        second_row = second_row_of(request)
        query = jnp.concatenate(
            [queries[rows_of(request), :], second_queries[rows_of(second_row), :]], axis=0
        )
        pick = picks[replica * REQUEST_COUNT + request].astype(jnp.float32)
        pick_rows[pl.ds(request, 1), :] = jnp.full((1, HEAD_WIDTH), pick, jnp.float32)
        pick_rows[pl.ds(REQUEST_COUNT + second_row, 1), :] = jnp.full(
            (1, HEAD_WIDTH), pick, jnp.float32
        )
        token = tokens[request]
        own = second_tokens[second_row]
        score = scores[request]
        token_score = jnp.sum(query * token[0:1], axis=1, keepdims=True) * scale
        own_score = jnp.sum(query * own[0:1], axis=1, keepdims=True) * scale
        own_score = jnp.where(second_half, own_score, -jnp.inf)
        row_max = jnp.max(score, axis=1, keepdims=True)
        row_max = jnp.maximum(row_max, jnp.maximum(token_score, own_score))
        weights = jnp.exp(score - row_max)
        token_weight = jnp.exp(token_score - row_max)
        own_weight = jnp.exp(own_score - row_max)
        row_sum = jnp.sum(weights, axis=1, keepdims=True) + token_weight + own_weight
        weights = pltpu.roll(weights / row_sum, 1, 1).astype(jnp.bfloat16)
        token_weight = (token_weight / row_sum).astype(jnp.bfloat16).astype(jnp.float32)
        own_weight = (own_weight / row_sum).astype(jnp.bfloat16).astype(jnp.float32)
        blended = jnp.dot(weights, held_of(request), preferred_element_type=jnp.float32)
        blended = blended + token_weight * token[1:2] + own_weight * own[1:2]
        attended[rows_of(request), :] = blended[0:GROUP]
        attended[rows_of(REQUEST_COUNT + second_row), :] = blended[GROUP : 2 * GROUP]

    unrolled = 8

    def for_requests(work):
        def some_requests(step, carry):
            for k in range(unrolled):
                work(step * unrolled + k)
            return carry

        lax.fori_loop(0, REQUEST_COUNT // unrolled, some_requests, 0)

    for_requests(score_request)
    for_requests(blend_request)

    rows = 2 * REQUEST_COUNT
    held = jnp.concatenate(
        [attended[pl.ds(h, rows, stride=GROUP), :] for h in range(GROUP)], axis=1
    ).astype(jnp.bfloat16)
    pick_all = pick_rows[...]
    picks_out[...] = pick_all
    wait_all(arrays[4:])
    low = jnp.zeros((rows, PADDED_RANK), jnp.float32)
    lane = lax.broadcasted_iota(jnp.int32, (rows, PADDED_RANK), 1)
    for slot in range(ADAPTER_COUNT):
        level = jnp.left_shift(jnp.int32(1), buckets[replica * ADAPTER_COUNT + slot])
        scale = 2.0 / level.astype(jnp.float32)
        part = jnp.dot(held, down[slot], preferred_element_type=jnp.float32)
        live = (pick_all == slot) & (lane < RANK_UNIT * level)
        low = jnp.where(live, part * scale, low)
    low = low.astype(jnp.bfloat16)

    def one_part(part, carry):
        weight_copy(part).wait()
        share = jnp.dot(held, weight[part], preferred_element_type=jnp.float32)
        shares_out[part, :, 0:width] = share.astype(jnp.bfloat16)
        shares_out[part, :, width:] = low
        return carry

    lax.fori_loop(0, parts, one_part, 0)


def attend(tables, pool, weight, query, token, second_query, second_token, arrived, down, up, parts):
    blocks, lengths, moving, picks, buckets = tables
    rows = 2 * REQUEST_COUNT
    width = weight.shape[1] // parts
    depth = weight.shape[0]
    return pl.pallas_call(
        attend_kernel,
        out_shape=(
            jax.ShapeDtypeStruct((parts, rows, width + PADDED_RANK), jnp.bfloat16),
            jax.ShapeDtypeStruct((rows, PADDED_RANK), jnp.float32),
            jax.ShapeDtypeStruct(up.shape, jnp.bfloat16),
        ),
        in_specs=[VMEM] + [ANY] * 13,
        out_specs=(VMEM,) * 3,
        scratch_shapes=[
            pltpu.SMEM(lengths.shape, jnp.int32),
            pltpu.SMEM(moving.shape, jnp.int32),
            pltpu.SMEM(buckets.shape, jnp.int32),
            pltpu.SMEM(picks.shape, jnp.int32),
            pltpu.SMEM(blocks.shape, jnp.int32),
            pltpu.VMEM(query.shape, jnp.bfloat16),
            pltpu.VMEM(token.shape, jnp.bfloat16),
            pltpu.VMEM(second_query.shape, jnp.bfloat16),
            pltpu.VMEM(second_token.shape, jnp.bfloat16),
            pltpu.VMEM(down.shape, jnp.bfloat16),
            pltpu.VMEM(pool.shape, jnp.bfloat16),
            pltpu.VMEM((parts, depth, width), jnp.bfloat16),
            pltpu.VMEM((REQUEST_COUNT * GROUP, HEAD_WIDTH), jnp.float32),
            pltpu.VMEM((REQUEST_COUNT * GROUP, HEAD_WIDTH), jnp.float32),
            pltpu.VMEM((REQUEST_COUNT, 8, HEAD_WIDTH), jnp.float32),
            pltpu.VMEM((REQUEST_COUNT, 8, HEAD_WIDTH), jnp.float32),
            pltpu.VMEM((rows * GROUP, HEAD_WIDTH), jnp.float32),
            pltpu.VMEM((REQUEST_COUNT, 2 * GROUP, CACHE_ROWS), jnp.float32),
            pltpu.VMEM((rows, HEAD_WIDTH), jnp.float32),
            pltpu.SemaphoreType.DMA((5,)),
            pltpu.SemaphoreType.DMA((6,)),
            pltpu.SemaphoreType.DMA((4,)),
            pltpu.SemaphoreType.DMA((parts,)),
        ],
        compiler_params=params(40),
        cost_estimate=cost(10**6, MIB),
        name="attend_project",
    )(
        arrived,
        lengths,
        moving,
        buckets,
        picks,
        blocks,
        pool,
        query,
        token,
        second_query,
        second_token,
        down,
        up,
        weight,
    )


def finish_kernel(shares_ref, picks_ref, up_ref, first_out, second_out, leaving_out):
    parts, rows, _ = shares_ref.shape
    width = first_out.shape[1]
    total = shares_ref[0].astype(jnp.float32)
    for part in range(1, parts):
        total = total + shares_ref[part].astype(jnp.float32)
    base, low = total[:, 0:width], total[:, width:]
    picks = picks_ref[...]
    for slot in range(ADAPTER_COUNT):
        rest = jnp.where(picks == slot, low, 0.0)
        pieces = []
        for _ in range(3):
            piece = rest.astype(jnp.bfloat16)
            rest = rest - piece.astype(jnp.float32)
            pieces.append(piece)
        stacked = jnp.concatenate(pieces, axis=0)
        part = jnp.dot(stacked, up_ref[slot], preferred_element_type=jnp.float32)
        base = base + (part[0:rows] + part[rows : 2 * rows] + part[2 * rows : 3 * rows])
    result = base.astype(jnp.bfloat16)
    first_out[...] = result[0:REQUEST_COUNT]
    second_out[...] = result[REQUEST_COUNT:]
    leaving_out[...] = base[REQUEST_COUNT + STAYING :].astype(jnp.bfloat16)


def finish(shares, picks, up):
    width = shares.shape[2] - PADDED_RANK
    return pl.pallas_call(
        finish_kernel,
        out_shape=(
            jax.ShapeDtypeStruct((REQUEST_COUNT, width), jnp.bfloat16),
            jax.ShapeDtypeStruct((REQUEST_COUNT, width), jnp.bfloat16),
            jax.ShapeDtypeStruct((MOVING_REQUESTS, width), jnp.bfloat16),
        ),
        in_specs=[VMEM] * 3,
        out_specs=(VMEM,) * 3,
        compiler_params=params(16),
        cost_estimate=cost(10**6, MIB),
        name="finish",
    )(shares, picks, up)


def swapped(mask):
    pairs = [(source, source ^ mask) for source in range(lax.axis_size("replica"))]
    return functools.partial(lax.ppermute, axis_name="replica", perm=pairs)


def branch(mask, tables, pool, weight, arrays, factors, moved_query, payload):
    query, token, second_query, second_token = arrays
    swap = swapped(mask) if mask else lambda value: value
    arrived = swap(moved_query)
    payload, arrived = lax.optimization_barrier((payload, arrived))
    units = swap(payload)
    shares, picks, held_up = attend(
        tables,
        pool,
        weight,
        query,
        token,
        second_query,
        second_token,
        arrived,
        *factors,
        lax.axis_size("tensor"),
    )
    shares = lax.all_to_all(shares, "tensor", 0, 0, tiled=True)
    first, second, leaving = finish(shares, picks, held_up)
    return first, second, swap(leaving), units


def keep(values):
    return values


def other_core(values):
    return tuple(swapped(1)(value) for value in values)


def shards(
    first_queries,
    first_key_value,
    second_queries,
    second_key_value,
    key_value_pool,
    request_blocks,
    lengths,
    moving_request_list,
    adapter_index,
    adapter_rank_bucket,
    replica_pair_mask,
    adapter_down_factors,
    adapter_up_factors,
    output_weight,
):
    tables = (
        request_blocks.T,
        lengths,
        moving_request_list,
        adapter_index,
        adapter_rank_bucket,
    )
    pool = key_value_pool.reshape(key_value_pool.shape[0], BLOCK_ROWS, HEAD_WIDTH)
    factors = (adapter_down_factors, adapter_up_factors)
    choice, moved_query, payload = prepare(
        tables,
        replica_pair_mask,
        pool,
        first_key_value,
        second_queries,
        second_key_value,
        *factors,
    )
    to_other_core = choice[1] == 1
    moved_query = lax.cond(to_other_core, swapped(1), lambda value: value, moved_query)
    arrays = (first_queries, first_key_value, second_queries, second_key_value)
    branches = [
        functools.partial(branch, mask) for mask in range(0, lax.axis_size("replica"), 2)
    ]
    first, second, rows, units = lax.switch(
        choice[0], branches, tables, pool, output_weight, arrays, factors, moved_query, payload
    )
    units, rows = lax.cond(to_other_core, other_core, keep, (units, rows))
    second, cache, down, up = unpack(tables, replica_pair_mask, units, second, rows, *factors)
    cache = cache.reshape(MOVING_REQUESTS, MAXB * BLOCK_TOKENS, 2, HEAD_WIDTH)
    return first, second, cache, down, up


def solution(mesh):
    placed = (
        P("replica", "tensor"),
        P("replica", None, "tensor"),
        P("replica", "tensor"),
        P("replica", None, "tensor"),
        P("replica", None, None, "tensor"),
        P(),
        P(),
        P(),
        P(),
        P(),
        P(),
        P("replica", "tensor", None),
        P("replica", None, "tensor"),
        P("tensor", None),
    )
    return jax.shard_map(
        shards,
        mesh=mesh,
        in_specs=placed,
        out_specs=(
            P("replica", "tensor"),
            P("replica", "tensor"),
            P("replica", None, None, "tensor"),
            P("replica", "tensor", None),
            P("replica", None, "tensor"),
        ),
        check_vma=False,
    )
```

```python
import functools

import jax
import jax.numpy as jnp
from jax import lax
from jax.experimental import pallas as pl
from jax.experimental.pallas import tpu as pltpu
from jax.sharding import PartitionSpec as P

HEAD_WIDTH = 128
GROUP = 8
PADDED_RANK = 128
REQUEST_COUNT = 16
MOVING_REQUESTS = 2
STAYING = REQUEST_COUNT - MOVING_REQUESTS
ADAPTER_COUNT = 2
BLOCK_TOKENS = 64
BLOCK_ROWS = 2 * BLOCK_TOKENS
MAXB = 8
CACHE_ROWS = MAXB * BLOCK_ROWS
MIB = 1 << 20

UNIT_ROWS = 128
RANK_UNIT = 16
ADAPTER_UNITS = PADDED_RANK // RANK_UNIT
MOST_UNITS = MOVING_REQUESTS * MAXB + 2 * ADAPTER_COUNT * ADAPTER_UNITS

ANY = pl.BlockSpec(memory_space=pl.ANY)
VMEM = pl.BlockSpec(memory_space=pltpu.VMEM)
SMEM = pl.BlockSpec(memory_space=pltpu.SMEM)


def params(mib):
    return pltpu.CompilerParams(vmem_limit_bytes=mib * MIB)


def cost(flops, moved):
    return pl.CostEstimate(flops=flops, bytes_accessed=moved, transcendentals=0)


def copies_of(pairs, sems):
    return [
        pltpu.make_async_copy(source, target, sems.at[place])
        for place, (source, target) in enumerate(pairs)
    ]


def start_all(copies):
    for copy in copies:
        copy.start()


def wait_all(copies):
    for copy in copies:
        copy.wait()


def unit_layout(replica, lengths, moving, buckets):
    counts = []
    for slot in range(MOVING_REQUESTS):
        request = moving[replica * MOVING_REQUESTS + slot]
        length = lengths[replica * REQUEST_COUNT + request]
        counts.append(lax.div(length, BLOCK_TOKENS) + 1)
    levels = [
        jnp.left_shift(jnp.int32(1), buckets[replica * ADAPTER_COUNT + slot])
        for slot in range(ADAPTER_COUNT)
    ]
    counts = counts + levels + levels
    starts, total = [], jnp.int32(0)
    for count in counts:
        starts.append(total)
        total = total + count
    return counts, starts, total


def pack_down(source, bucket):
    rows = UNIT_ROWS << bucket
    lanes = RANK_UNIT << bucket
    lane = lax.broadcasted_iota(jnp.int32, (rows, PADDED_RANK), 1)
    packed = jnp.zeros((rows, PADDED_RANK), jnp.float32)
    for group in range(PADDED_RANK // lanes):
        part = source[group * rows : (group + 1) * rows, :].astype(jnp.float32)
        if group:
            part = pltpu.roll(part, group * lanes, 1)
        here = (lane >= group * lanes) & (lane < (group + 1) * lanes)
        packed = jnp.where(here, part, packed)
    return packed.astype(jnp.bfloat16)


def prepare_kernel(
    lengths_ref,
    moving_ref,
    buckets_ref,
    blocks_ref,
    pool_ref,
    token_ref,
    query_ref,
    second_token_ref,
    down_ref,
    up_ref,
    query_out,
    units,
    lengths,
    moving,
    buckets,
    blocks,
    tokens,
    queries,
    second_tokens,
    down,
    up,
    table_sems,
    sems,
    block_sems,
):
    replica = lax.axis_index("replica")
    tables = copies_of(
        [
            (lengths_ref, lengths),
            (moving_ref, moving),
            (buckets_ref, buckets),
            (blocks_ref, blocks),
        ],
        table_sems,
    )
    arrays = copies_of(
        [
            (query_ref, queries),
            (second_token_ref, second_tokens),
            (token_ref, tokens),
            (down_ref, down),
            (up_ref, up),
        ],
        sems,
    )
    start_all(tables)
    start_all(arrays)
    wait_all(tables)
    counts, starts, _ = unit_layout(replica, lengths, moving, buckets)
    requests = [moving[replica * MOVING_REQUESTS + slot] for slot in range(MOVING_REQUESTS)]

    def block_copy(slot, block):
        return pltpu.make_async_copy(
            pool_ref.at[blocks[block, replica * REQUEST_COUNT + requests[slot]]],
            units.at[starts[slot] + block],
            block_sems.at[slot, block],
        )

    for slot in range(MOVING_REQUESTS):
        for block in range(MAXB):
            pl.when(block < counts[slot])(lambda s=slot, b=block: block_copy(s, b).start())

    wait_all(arrays[:3])
    for slot in range(MOVING_REQUESTS):
        row = STAYING + slot
        heads = [
            queries[row : row + 1, h * HEAD_WIDTH : (h + 1) * HEAD_WIDTH].astype(jnp.float32)
            for h in range(GROUP)
        ]
        own = second_tokens[row].astype(jnp.float32)
        padding = jnp.zeros((16 - GROUP - 2, HEAD_WIDTH), jnp.float32)
        query_out[slot] = jnp.concatenate(heads + [own, padding], axis=0).astype(jnp.bfloat16)
    wait_all(arrays[3:])
    for slot in range(ADAPTER_COUNT):
        bucket = buckets[replica * ADAPTER_COUNT + slot]
        level = jnp.left_shift(jnp.int32(1), bucket)
        scale = 2.0 / level.astype(jnp.float32)
        base = starts[MOVING_REQUESTS + slot]
        for kind in range(4):

            @pl.when(bucket == kind)
            def _(kind=kind, slot=slot, base=base):
                packed = pack_down(down.at[slot], kind)
                for unit in range(1 << kind):
                    units[base + unit] = packed[unit * UNIT_ROWS : (unit + 1) * UNIT_ROWS]

        base = starts[MOVING_REQUESTS + ADAPTER_COUNT + slot]

        def up_unit(unit, carry, slot=slot, base=base, scale=scale):
            ranks = pl.ds(pl.multiple_of(unit * RANK_UNIT, RANK_UNIT), RANK_UNIT)
            part = (up[slot, ranks, :].astype(jnp.float32) * scale).astype(jnp.bfloat16)
            for column in range(UNIT_ROWS // RANK_UNIT):
                units[base + unit, column * RANK_UNIT : (column + 1) * RANK_UNIT, :] = part[
                    :, column * HEAD_WIDTH : (column + 1) * HEAD_WIDTH
                ]
            return carry

        lax.fori_loop(0, level, up_unit, 0)
    for slot in range(MOVING_REQUESTS):
        for block in range(MAXB):
            pl.when(block < counts[slot])(lambda s=slot, b=block: block_copy(s, b).wait())
        length = lengths[replica * REQUEST_COUNT + requests[slot]]
        token = tokens[requests[slot]].astype(jnp.float32)
        row = lax.broadcasted_iota(jnp.int32, (UNIT_ROWS, HEAD_WIDTH), 0)
        position = jnp.right_shift(row, 1) + (counts[slot] - 1) * BLOCK_TOKENS
        own = jnp.where(jnp.bitwise_and(row, 1) == 0, token[0:1], token[1:2])
        last = starts[slot] + counts[slot] - 1
        held = units[last].astype(jnp.float32)
        kept = jnp.where(position < length, held, jnp.where(position == length, own, 0.0))
        units[last] = kept.astype(jnp.bfloat16)


def prepare(tables, pool, token, query, second_token, down, up):
    blocks, lengths, moving, _, buckets = tables
    return pl.pallas_call(
        prepare_kernel,
        out_shape=(
            jax.ShapeDtypeStruct((MOVING_REQUESTS, 16, HEAD_WIDTH), jnp.bfloat16),
            jax.ShapeDtypeStruct((MOST_UNITS, UNIT_ROWS, HEAD_WIDTH), jnp.bfloat16),
        ),
        in_specs=[ANY] * 10,
        out_specs=(VMEM, VMEM),
        scratch_shapes=[
            pltpu.SMEM(lengths.shape, jnp.int32),
            pltpu.SMEM(moving.shape, jnp.int32),
            pltpu.SMEM(buckets.shape, jnp.int32),
            pltpu.SMEM(blocks.shape, jnp.int32),
            pltpu.VMEM(token.shape, jnp.bfloat16),
            pltpu.VMEM(query.shape, jnp.bfloat16),
            pltpu.VMEM(second_token.shape, jnp.bfloat16),
            pltpu.VMEM(down.shape, jnp.bfloat16),
            pltpu.VMEM(up.shape, jnp.bfloat16),
            pltpu.SemaphoreType.DMA((4,)),
            pltpu.SemaphoreType.DMA((5,)),
            pltpu.SemaphoreType.DMA((MOVING_REQUESTS, MAXB)),
        ],
        compiler_params=params(16),
        cost_estimate=cost(10**6, 3 * MIB),
        name="prepare",
    )(lengths, moving, buckets, blocks, pool, token, query, second_token, down, up)


def unpack_kernel(
    lengths_ref,
    moving_ref,
    buckets_ref,
    mask_ref,
    units,
    second_ref,
    rows_ref,
    second_out,
    cache_out,
    down_out,
    up_out,
    lengths,
    moving,
    buckets,
    mask,
    zeros,
    down,
    up,
    table_sems,
    block_sems,
    out_sems,
):
    tables = copies_of(
        [
            (lengths_ref, lengths),
            (moving_ref, moving),
            (buckets_ref, buckets),
            (mask_ref, mask),
        ],
        table_sems,
    )
    start_all(tables)
    zeros[...] = jnp.zeros_like(zeros)
    kept = second_ref[0:STAYING, :].astype(jnp.float32)
    came = rows_ref[...].astype(jnp.float32)
    second_out[...] = jnp.concatenate([kept, came], axis=0).astype(jnp.bfloat16)
    wait_all(tables)
    mate = jnp.bitwise_xor(lax.axis_index("replica"), mask[0])
    counts, starts, _ = unit_layout(mate, lengths, moving, buckets)

    def block_copy(slot, block, source):
        return pltpu.make_async_copy(
            source,
            cache_out.at[slot, pl.ds(block * BLOCK_ROWS, BLOCK_ROWS)],
            block_sems.at[slot, block],
        )

    for slot in range(MOVING_REQUESTS):
        for block in range(MAXB):
            pl.when(block < counts[slot])(
                lambda s=slot, b=block: block_copy(s, b, units.at[starts[s] + b]).start()
            )
            pl.when(block >= counts[slot])(lambda s=slot, b=block: block_copy(s, b, zeros).start())
    outs = []
    for slot in range(ADAPTER_COUNT):
        bucket = buckets[mate * ADAPTER_COUNT + slot]
        base = starts[MOVING_REQUESTS + slot]
        for kind in range(4):

            @pl.when(bucket == kind)
            def _(kind=kind, slot=slot, base=base):
                rows = UNIT_ROWS << kind
                lanes = RANK_UNIT << kind
                packed = jnp.concatenate(
                    [units[base + unit] for unit in range(1 << kind)], axis=0
                ).astype(jnp.float32)
                lane = lax.broadcasted_iota(jnp.int32, packed.shape, 1)
                for group in range(PADDED_RANK // lanes):
                    part = packed
                    if group:
                        part = pltpu.roll(part, PADDED_RANK - group * lanes, 1)
                    part = jnp.where(lane < lanes, part, 0.0).astype(jnp.bfloat16)
                    down[slot, group * rows : (group + 1) * rows, :] = part

        outs.append(pltpu.make_async_copy(down.at[slot], down_out.at[slot], out_sems.at[0, slot]))
        outs[-1].start()
        level = counts[MOVING_REQUESTS + slot]
        base = starts[MOVING_REQUESTS + ADAPTER_COUNT + slot]

        def up_unit(unit, carry, slot=slot, base=base, level=level):
            ranks = pl.ds(pl.multiple_of(unit * RANK_UNIT, RANK_UNIT), RANK_UNIT)
            held = units[base + jnp.minimum(unit, level - 1)]
            for column in range(UNIT_ROWS // RANK_UNIT):
                part = held[column * RANK_UNIT : (column + 1) * RANK_UNIT]
                up[slot, ranks, column * HEAD_WIDTH : (column + 1) * HEAD_WIDTH] = jnp.where(
                    unit < level, part, jnp.zeros_like(part)
                )
            return carry

        lax.fori_loop(0, ADAPTER_UNITS, up_unit, 0)
        outs.append(pltpu.make_async_copy(up.at[slot], up_out.at[slot], out_sems.at[1, slot]))
        outs[-1].start()
    for slot in range(MOVING_REQUESTS):
        for block in range(MAXB):
            block_copy(slot, block, zeros).wait()
    wait_all(outs)


def unpack(tables, mask, units, second, rows, down, up):
    _, lengths, moving, _, buckets = tables
    return pl.pallas_call(
        unpack_kernel,
        out_shape=(
            jax.ShapeDtypeStruct(second.shape, jnp.bfloat16),
            jax.ShapeDtypeStruct((MOVING_REQUESTS, CACHE_ROWS, HEAD_WIDTH), jnp.bfloat16),
            jax.ShapeDtypeStruct(down.shape, jnp.bfloat16),
            jax.ShapeDtypeStruct(up.shape, jnp.bfloat16),
        ),
        in_specs=[ANY] * 4 + [VMEM] * 3,
        out_specs=(VMEM,) + (ANY,) * 3,
        scratch_shapes=[
            pltpu.SMEM(lengths.shape, jnp.int32),
            pltpu.SMEM(moving.shape, jnp.int32),
            pltpu.SMEM(buckets.shape, jnp.int32),
            pltpu.SMEM(mask.shape, jnp.int32),
            pltpu.VMEM((BLOCK_ROWS, HEAD_WIDTH), jnp.bfloat16),
            pltpu.VMEM(down.shape, jnp.bfloat16),
            pltpu.VMEM(up.shape, jnp.bfloat16),
            pltpu.SemaphoreType.DMA((4,)),
            pltpu.SemaphoreType.DMA((MOVING_REQUESTS, MAXB)),
            pltpu.SemaphoreType.DMA((2, ADAPTER_COUNT)),
        ],
        compiler_params=params(16),
        cost_estimate=cost(10**6, 3 * MIB),
        name="unpack",
    )(lengths, moving, buckets, mask, units, second, rows)


def attend_kernel(
    arrived_ref,
    lengths_ref,
    moving_ref,
    buckets_ref,
    picks_ref,
    blocks_ref,
    pool_ref,
    query_ref,
    token_ref,
    second_query_ref,
    second_token_ref,
    down_ref,
    up_ref,
    weight_ref,
    shares_out,
    picks_out,
    up_out,
    lengths,
    moving,
    buckets,
    picks,
    blocks,
    raw_query,
    raw_token,
    raw_second_query,
    raw_second_token,
    down,
    pool,
    weight,
    queries,
    second_queries,
    tokens,
    second_tokens,
    attended,
    scores,
    pick_rows,
    table_sems,
    sems,
    pool_sems,
    weight_sems,
):
    replica = lax.axis_index("replica")
    parts = shares_out.shape[0]
    width = weight_ref.shape[1] // parts
    pool_parts = pool_sems.shape[0]
    per_part = pool_ref.shape[0] // pool_parts

    def pool_copy(part):
        where = pl.ds(part * per_part, per_part)
        return pltpu.make_async_copy(pool_ref.at[where], pool.at[where], pool_sems.at[part])

    def weight_copy(part):
        columns = pl.ds(pl.multiple_of(part * width, width), width)
        return pltpu.make_async_copy(
            weight_ref.at[:, columns], weight.at[part], weight_sems.at[part]
        )

    tables = copies_of(
        [
            (lengths_ref, lengths),
            (moving_ref, moving),
            (buckets_ref, buckets),
            (picks_ref, picks),
            (blocks_ref, blocks),
        ],
        table_sems,
    )
    arrays = copies_of(
        [
            (query_ref, raw_query),
            (token_ref, raw_token),
            (second_query_ref, raw_second_query),
            (second_token_ref, raw_second_token),
            (down_ref, down),
            (up_ref, up_out),
        ],
        sems,
    )
    start_all(tables)
    start_all(arrays[:4])
    for part in range(pool_parts):
        pool_copy(part).start()
    wait_all(arrays[:4])
    for h in range(GROUP):
        columns = slice(h * HEAD_WIDTH, (h + 1) * HEAD_WIDTH)
        rows = pl.ds(h, REQUEST_COUNT, stride=GROUP)
        queries[rows, :] = raw_query[:, columns].astype(jnp.float32)
        second_queries[rows, :] = raw_second_query[:, columns].astype(jnp.float32)
    tokens[:, 0:2, :] = raw_token[...].astype(jnp.float32)
    second_tokens[:, 0:2, :] = raw_second_token[...].astype(jnp.float32)
    for slot in range(MOVING_REQUESTS):
        row = STAYING + slot
        arrived = arrived_ref[slot].astype(jnp.float32)
        second_queries[row * GROUP : (row + 1) * GROUP, :] = arrived[0:GROUP]
        second_tokens[row, 0:2, :] = arrived[GROUP : GROUP + 2]
    wait_all(tables)
    for part in range(pool_parts):
        pool_copy(part).wait()
    for part in range(parts):
        weight_copy(part).start()
    start_all(arrays[4:])

    leaving = [moving[replica * MOVING_REQUESTS + slot] for slot in range(MOVING_REQUESTS)]
    lane = lax.broadcasted_iota(jnp.int32, (2 * GROUP, CACHE_ROWS), 1)
    position = jnp.right_shift(lane, 1)
    is_key = jnp.bitwise_and(lane, 1) == 0
    second_half = lax.broadcasted_iota(jnp.int32, (2 * GROUP, 1), 0) >= GROUP

    scale = HEAD_WIDTH ** (-0.5)

    def second_row_of(request):
        second_row = request
        for slot in range(MOVING_REQUESTS):
            second_row = second_row - (leaving[slot] < request).astype(jnp.int32)
        for slot in range(MOVING_REQUESTS):
            second_row = jnp.where(leaving[slot] == request, STAYING + slot, second_row)
        return second_row

    def rows_of(row):
        return pl.ds(pl.multiple_of(row * GROUP, GROUP), GROUP)

    def held_of(request):
        return jnp.concatenate([pool[blocks[b, replica * REQUEST_COUNT + request]] for b in range(MAXB)], axis=0)

    def score_request(request):
        second_row = second_row_of(request)
        query = jnp.concatenate(
            [queries[rows_of(request), :], second_queries[rows_of(second_row), :]], axis=0
        )
        length = lengths[replica * REQUEST_COUNT + request]
        dots = lax.dot_general(
            query.astype(jnp.bfloat16),
            held_of(request),
            (((1,), (1,)), ((), ())),
            preferred_element_type=jnp.float32,
        )
        scores[request] = jnp.where(is_key & (position < length), dots * scale, -jnp.inf)

    def blend_request(request):
        second_row = second_row_of(request)
        query = jnp.concatenate(
            [queries[rows_of(request), :], second_queries[rows_of(second_row), :]], axis=0
        )
        pick = picks[replica * REQUEST_COUNT + request].astype(jnp.float32)
        pick_rows[pl.ds(request, 1), :] = jnp.full((1, HEAD_WIDTH), pick, jnp.float32)
        pick_rows[pl.ds(REQUEST_COUNT + second_row, 1), :] = jnp.full(
            (1, HEAD_WIDTH), pick, jnp.float32
        )
        token = tokens[request]
        own = second_tokens[second_row]
        score = scores[request]
        token_score = jnp.sum(query * token[0:1], axis=1, keepdims=True) * scale
        own_score = jnp.sum(query * own[0:1], axis=1, keepdims=True) * scale
        own_score = jnp.where(second_half, own_score, -jnp.inf)
        row_max = jnp.max(score, axis=1, keepdims=True)
        row_max = jnp.maximum(row_max, jnp.maximum(token_score, own_score))
        weights = jnp.exp(score - row_max)
        token_weight = jnp.exp(token_score - row_max)
        own_weight = jnp.exp(own_score - row_max)
        row_sum = jnp.sum(weights, axis=1, keepdims=True) + token_weight + own_weight
        weights = pltpu.roll(weights / row_sum, 1, 1).astype(jnp.bfloat16)
        token_weight = (token_weight / row_sum).astype(jnp.bfloat16).astype(jnp.float32)
        own_weight = (own_weight / row_sum).astype(jnp.bfloat16).astype(jnp.float32)
        blended = jnp.dot(weights, held_of(request), preferred_element_type=jnp.float32)
        blended = blended + token_weight * token[1:2] + own_weight * own[1:2]
        attended[rows_of(request), :] = blended[0:GROUP]
        attended[rows_of(REQUEST_COUNT + second_row), :] = blended[GROUP : 2 * GROUP]

    unrolled = 8

    def for_requests(work):
        def some_requests(step, carry):
            for k in range(unrolled):
                work(step * unrolled + k)
            return carry

        lax.fori_loop(0, REQUEST_COUNT // unrolled, some_requests, 0)

    for_requests(score_request)
    for_requests(blend_request)

    rows = 2 * REQUEST_COUNT
    held = jnp.concatenate(
        [attended[pl.ds(h, rows, stride=GROUP), :] for h in range(GROUP)], axis=1
    ).astype(jnp.bfloat16)
    pick_all = pick_rows[...]
    picks_out[...] = pick_all
    wait_all(arrays[4:])
    low = jnp.zeros((rows, PADDED_RANK), jnp.float32)
    lane = lax.broadcasted_iota(jnp.int32, (rows, PADDED_RANK), 1)
    for slot in range(ADAPTER_COUNT):
        level = jnp.left_shift(jnp.int32(1), buckets[replica * ADAPTER_COUNT + slot])
        scale = 2.0 / level.astype(jnp.float32)
        part = jnp.dot(held, down[slot], preferred_element_type=jnp.float32)
        live = (pick_all == slot) & (lane < RANK_UNIT * level)
        low = jnp.where(live, part * scale, low)
    low = low.astype(jnp.bfloat16)

    def one_part(part, carry):
        weight_copy(part).wait()
        share = jnp.dot(held, weight[part], preferred_element_type=jnp.float32)
        shares_out[part, :, 0:width] = share.astype(jnp.bfloat16)
        shares_out[part, :, width:] = low
        return carry

    lax.fori_loop(0, parts, one_part, 0)


def attend(tables, pool, weight, query, token, second_query, second_token, arrived, down, up, parts):
    blocks, lengths, moving, picks, buckets = tables
    rows = 2 * REQUEST_COUNT
    width = weight.shape[1] // parts
    depth = weight.shape[0]
    return pl.pallas_call(
        attend_kernel,
        out_shape=(
            jax.ShapeDtypeStruct((parts, rows, width + PADDED_RANK), jnp.bfloat16),
            jax.ShapeDtypeStruct((rows, PADDED_RANK), jnp.float32),
            jax.ShapeDtypeStruct(up.shape, jnp.bfloat16),
        ),
        in_specs=[VMEM] + [ANY] * 13,
        out_specs=(VMEM,) * 3,
        scratch_shapes=[
            pltpu.SMEM(lengths.shape, jnp.int32),
            pltpu.SMEM(moving.shape, jnp.int32),
            pltpu.SMEM(buckets.shape, jnp.int32),
            pltpu.SMEM(picks.shape, jnp.int32),
            pltpu.SMEM(blocks.shape, jnp.int32),
            pltpu.VMEM(query.shape, jnp.bfloat16),
            pltpu.VMEM(token.shape, jnp.bfloat16),
            pltpu.VMEM(second_query.shape, jnp.bfloat16),
            pltpu.VMEM(second_token.shape, jnp.bfloat16),
            pltpu.VMEM(down.shape, jnp.bfloat16),
            pltpu.VMEM(pool.shape, jnp.bfloat16),
            pltpu.VMEM((parts, depth, width), jnp.bfloat16),
            pltpu.VMEM((REQUEST_COUNT * GROUP, HEAD_WIDTH), jnp.float32),
            pltpu.VMEM((REQUEST_COUNT * GROUP, HEAD_WIDTH), jnp.float32),
            pltpu.VMEM((REQUEST_COUNT, 8, HEAD_WIDTH), jnp.float32),
            pltpu.VMEM((REQUEST_COUNT, 8, HEAD_WIDTH), jnp.float32),
            pltpu.VMEM((rows * GROUP, HEAD_WIDTH), jnp.float32),
            pltpu.VMEM((REQUEST_COUNT, 2 * GROUP, CACHE_ROWS), jnp.float32),
            pltpu.VMEM((rows, HEAD_WIDTH), jnp.float32),
            pltpu.SemaphoreType.DMA((5,)),
            pltpu.SemaphoreType.DMA((6,)),
            pltpu.SemaphoreType.DMA((4,)),
            pltpu.SemaphoreType.DMA((parts,)),
        ],
        compiler_params=params(40),
        cost_estimate=cost(10**6, MIB),
        name="attend_project",
    )(
        arrived,
        lengths,
        moving,
        buckets,
        picks,
        blocks,
        pool,
        query,
        token,
        second_query,
        second_token,
        down,
        up,
        weight,
    )


def merge_kernel(shares_ref, send_out, keep_out):
    parts, near, _, _ = shares_ref.shape
    own = jnp.bitwise_and(lax.axis_index("tensor"), near - 1)

    def total(place):
        held = shares_ref[0, place].astype(jnp.float32)
        for part in range(1, parts):
            held = held + shares_ref[part, place].astype(jnp.float32)
        return held

    keep_out[...] = total(own)
    send_out[...] = total(near - 1 - own).astype(jnp.bfloat16)


def merge(shares):
    return pl.pallas_call(
        merge_kernel,
        out_shape=(
            jax.ShapeDtypeStruct(shares.shape[2:], jnp.bfloat16),
            jax.ShapeDtypeStruct(shares.shape[2:], jnp.float32),
        ),
        in_specs=[VMEM],
        out_specs=(VMEM,) * 2,
        compiler_params=params(16),
        cost_estimate=cost(10**6, MIB),
        name="merge",
    )(shares)


def finish_kernel(*refs):
    *shares, picks_ref, up_ref, first_out, second_out, leaving_out = refs
    rows = picks_ref.shape[0]
    width = first_out.shape[1]
    total = jnp.zeros((rows, width + PADDED_RANK), jnp.float32)
    for share in shares:
        pieces = [share[part] for part in range(share.shape[0])] if share.ndim == 3 else [share[...]]
        for piece in pieces:
            total = total + piece.astype(jnp.float32)
    base, low = total[:, 0:width], total[:, width:]
    picks = picks_ref[...]
    for slot in range(ADAPTER_COUNT):
        rest = jnp.where(picks == slot, low, 0.0)
        pieces = []
        for _ in range(3):
            piece = rest.astype(jnp.bfloat16)
            rest = rest - piece.astype(jnp.float32)
            pieces.append(piece)
        stacked = jnp.concatenate(pieces, axis=0)
        part = jnp.dot(stacked, up_ref[slot], preferred_element_type=jnp.float32)
        base = base + (part[0:rows] + part[rows : 2 * rows] + part[2 * rows : 3 * rows])
    result = base.astype(jnp.bfloat16)
    first_out[...] = result[0:REQUEST_COUNT]
    second_out[...] = result[REQUEST_COUNT:]
    leaving_out[...] = base[REQUEST_COUNT + STAYING :].astype(jnp.bfloat16)


def finish(shares, picks, up):
    width = shares[0].shape[-1] - PADDED_RANK
    return pl.pallas_call(
        finish_kernel,
        out_shape=(
            jax.ShapeDtypeStruct((REQUEST_COUNT, width), jnp.bfloat16),
            jax.ShapeDtypeStruct((REQUEST_COUNT, width), jnp.bfloat16),
            jax.ShapeDtypeStruct((MOVING_REQUESTS, width), jnp.bfloat16),
        ),
        in_specs=[VMEM] * (len(shares) + 2),
        out_specs=(VMEM,) * 3,
        compiler_params=params(16),
        cost_estimate=cost(10**6, MIB),
        name="finish",
    )(*shares, picks, up)


def swapped(mask):
    pairs = [(source, source ^ mask) for source in range(lax.axis_size("replica"))]
    return functools.partial(lax.ppermute, axis_name="replica", perm=pairs)


def sum_along_y(shares):
    parts, near = shares.shape[0], 2
    shares = shares.reshape(parts // near, near, *shares.shape[1:])
    groups = [list(range(start, parts, near)) for start in range(near)]
    shares = lax.all_to_all(shares, "tensor", 0, 0, tiled=True, axis_index_groups=groups)
    send, kept = merge(shares)
    pairs = [(source, source ^ 1) for source in range(parts)]
    return lax.ppermute(send, "tensor", pairs), kept


def branch(mask, tables, pool, weight, arrays, factors, moved_query, payload):
    query, token, second_query, second_token = arrays
    swap = swapped(mask) if mask else lambda value: value
    arrived = swap(moved_query)
    payload, arrived = lax.optimization_barrier((payload, arrived))
    units = swap(payload)
    shares, picks, held_up = attend(
        tables,
        pool,
        weight,
        query,
        token,
        second_query,
        second_token,
        arrived,
        *factors,
        lax.axis_size("tensor"),
    )
    if mask >= lax.axis_size("replica") // 2:
        shares = sum_along_y(shares)
    else:
        shares = (lax.all_to_all(shares, "tensor", 0, 0, tiled=True),)
    first, second, leaving = finish(shares, picks, held_up)
    return first, second, swap(leaving), units


def keep(values):
    return values


def other_core(values):
    return tuple(swapped(1)(value) for value in values)


def shards(
    first_queries,
    first_key_value,
    second_queries,
    second_key_value,
    key_value_pool,
    request_blocks,
    lengths,
    moving_request_list,
    adapter_index,
    adapter_rank_bucket,
    replica_pair_mask,
    adapter_down_factors,
    adapter_up_factors,
    output_weight,
):
    tables = (
        request_blocks.T,
        lengths,
        moving_request_list,
        adapter_index,
        adapter_rank_bucket,
    )
    pool = key_value_pool.reshape(key_value_pool.shape[0], BLOCK_ROWS, HEAD_WIDTH)
    factors = (adapter_down_factors, adapter_up_factors)
    moved_query, payload = prepare(
        tables,
        pool,
        first_key_value,
        second_queries,
        second_key_value,
        *factors,
    )
    mask = replica_pair_mask[0]
    to_other_core = jnp.bitwise_and(mask, 1) == 1
    moved_query = lax.cond(to_other_core, swapped(1), lambda value: value, moved_query)
    arrays = (first_queries, first_key_value, second_queries, second_key_value)
    branches = [
        functools.partial(branch, mask) for mask in range(0, lax.axis_size("replica"), 2)
    ]
    first, second, rows, units = lax.switch(
        jnp.right_shift(mask, 1), branches, tables, pool, output_weight, arrays, factors, moved_query, payload
    )
    units, rows = lax.cond(to_other_core, other_core, keep, (units, rows))
    second, cache, down, up = unpack(tables, replica_pair_mask, units, second, rows, *factors)
    cache = cache.reshape(MOVING_REQUESTS, MAXB * BLOCK_TOKENS, 2, HEAD_WIDTH)
    return first, second, cache, down, up


def solution(mesh):
    placed = (
        P("replica", "tensor"),
        P("replica", None, "tensor"),
        P("replica", "tensor"),
        P("replica", None, "tensor"),
        P("replica", None, None, "tensor"),
        P(),
        P(),
        P(),
        P(),
        P(),
        P(),
        P("replica", "tensor", None),
        P("replica", None, "tensor"),
        P("tensor", None),
    )
    return jax.shard_map(
        shards,
        mesh=mesh,
        in_specs=placed,
        out_specs=(
            P("replica", "tensor"),
            P("replica", "tensor"),
            P("replica", None, None, "tensor"),
            P("replica", "tensor", None),
            P("replica", None, "tensor"),
        ),
        check_vma=False,
    )
```

```python
import functools

import jax
import jax.numpy as jnp
from jax import lax
from jax.experimental import pallas as pl
from jax.experimental.pallas import tpu as pltpu
from jax.sharding import PartitionSpec as P

HEAD_WIDTH = 128
GROUP = 8
PADDED_RANK = 128
REQUEST_COUNT = 16
MOVING_REQUESTS = 2
STAYING = REQUEST_COUNT - MOVING_REQUESTS
ADAPTER_COUNT = 2
BLOCK_TOKENS = 64
BLOCK_ROWS = 2 * BLOCK_TOKENS
MAXB = 8
CACHE_ROWS = MAXB * BLOCK_ROWS
MIB = 1 << 20

UNIT_ROWS = 128
RANK_UNIT = 16
ADAPTER_UNITS = PADDED_RANK // RANK_UNIT
MOST_UNITS = MOVING_REQUESTS * MAXB + 2 * ADAPTER_COUNT * ADAPTER_UNITS
FIRST_UNITS = 40

ANY = pl.BlockSpec(memory_space=pl.ANY)
VMEM = pl.BlockSpec(memory_space=pltpu.VMEM)
SMEM = pl.BlockSpec(memory_space=pltpu.SMEM)


def params(mib):
    return pltpu.CompilerParams(vmem_limit_bytes=mib * MIB)


def cost(flops, moved):
    return pl.CostEstimate(flops=flops, bytes_accessed=moved, transcendentals=0)


def copies_of(pairs, sems):
    return [
        pltpu.make_async_copy(source, target, sems.at[place])
        for place, (source, target) in enumerate(pairs)
    ]


def start_all(copies):
    for copy in copies:
        copy.start()


def wait_all(copies):
    for copy in copies:
        copy.wait()


def unit_layout(replica, lengths, moving, buckets):
    counts = []
    for slot in range(MOVING_REQUESTS):
        request = moving[replica * MOVING_REQUESTS + slot]
        length = lengths[replica * REQUEST_COUNT + request]
        counts.append(lax.div(length, BLOCK_TOKENS) + 1)
    levels = [
        jnp.left_shift(jnp.int32(1), buckets[replica * ADAPTER_COUNT + slot])
        for slot in range(ADAPTER_COUNT)
    ]
    counts = counts + levels + levels
    starts, total = [], jnp.int32(0)
    for count in counts:
        starts.append(total)
        total = total + count
    return counts, starts, total


def pack_down(source, bucket):
    rows = UNIT_ROWS << bucket
    lanes = RANK_UNIT << bucket
    lane = lax.broadcasted_iota(jnp.int32, (rows, PADDED_RANK), 1)
    packed = jnp.zeros((rows, PADDED_RANK), jnp.float32)
    for group in range(PADDED_RANK // lanes):
        part = source[group * rows : (group + 1) * rows, :].astype(jnp.float32)
        if group:
            part = pltpu.roll(part, group * lanes, 1)
        here = (lane >= group * lanes) & (lane < (group + 1) * lanes)
        packed = jnp.where(here, part, packed)
    return packed.astype(jnp.bfloat16)


def prepare_kernel(
    lengths_ref,
    moving_ref,
    buckets_ref,
    blocks_ref,
    pool_ref,
    token_ref,
    query_ref,
    second_token_ref,
    down_ref,
    up_ref,
    query_out,
    units,
    late_units,
    lengths,
    moving,
    buckets,
    blocks,
    tokens,
    queries,
    second_tokens,
    down,
    up,
    table_sems,
    sems,
    block_sems,
):
    replica = lax.axis_index("replica")
    tables = copies_of(
        [
            (lengths_ref, lengths),
            (moving_ref, moving),
            (buckets_ref, buckets),
            (blocks_ref, blocks),
        ],
        table_sems,
    )
    arrays = copies_of(
        [
            (query_ref, queries),
            (second_token_ref, second_tokens),
            (token_ref, tokens),
            (down_ref, down),
            (up_ref, up),
        ],
        sems,
    )
    start_all(tables)
    start_all(arrays)
    wait_all(tables)
    counts, starts, _ = unit_layout(replica, lengths, moving, buckets)
    requests = [moving[replica * MOVING_REQUESTS + slot] for slot in range(MOVING_REQUESTS)]

    def block_copy(slot, block):
        return pltpu.make_async_copy(
            pool_ref.at[blocks[block, replica * REQUEST_COUNT + requests[slot]]],
            units.at[starts[slot] + block],
            block_sems.at[slot, block],
        )

    for slot in range(MOVING_REQUESTS):
        for block in range(MAXB):
            pl.when(block < counts[slot])(lambda s=slot, b=block: block_copy(s, b).start())

    wait_all(arrays[:3])
    for slot in range(MOVING_REQUESTS):
        row = STAYING + slot
        heads = [
            queries[row : row + 1, h * HEAD_WIDTH : (h + 1) * HEAD_WIDTH].astype(jnp.float32)
            for h in range(GROUP)
        ]
        own = second_tokens[row].astype(jnp.float32)
        padding = jnp.zeros((16 - GROUP - 2, HEAD_WIDTH), jnp.float32)
        query_out[slot] = jnp.concatenate(heads + [own, padding], axis=0).astype(jnp.bfloat16)
    wait_all(arrays[3:])
    for slot in range(ADAPTER_COUNT):
        bucket = buckets[replica * ADAPTER_COUNT + slot]
        level = jnp.left_shift(jnp.int32(1), bucket)
        scale = 2.0 / level.astype(jnp.float32)
        base = starts[MOVING_REQUESTS + slot]
        for kind in range(4):

            @pl.when(bucket == kind)
            def _(kind=kind, slot=slot, base=base):
                packed = pack_down(down.at[slot], kind)
                for unit in range(1 << kind):
                    units[base + unit] = packed[unit * UNIT_ROWS : (unit + 1) * UNIT_ROWS]

        base = starts[MOVING_REQUESTS + ADAPTER_COUNT + slot]

        def up_unit(unit, carry, slot=slot, base=base, scale=scale):
            ranks = pl.ds(pl.multiple_of(unit * RANK_UNIT, RANK_UNIT), RANK_UNIT)
            part = (up[slot, ranks, :].astype(jnp.float32) * scale).astype(jnp.bfloat16)
            place = base + unit

            def put(target, where):
                for column in range(UNIT_ROWS // RANK_UNIT):
                    target[where, column * RANK_UNIT : (column + 1) * RANK_UNIT, :] = part[
                        :, column * HEAD_WIDTH : (column + 1) * HEAD_WIDTH
                    ]

            pl.when(place < FIRST_UNITS)(lambda: put(units, place))
            pl.when(place >= FIRST_UNITS)(lambda: put(late_units, place - FIRST_UNITS))
            return carry

        lax.fori_loop(0, level, up_unit, 0)
    for slot in range(MOVING_REQUESTS):
        for block in range(MAXB):
            pl.when(block < counts[slot])(lambda s=slot, b=block: block_copy(s, b).wait())
        length = lengths[replica * REQUEST_COUNT + requests[slot]]
        token = tokens[requests[slot]].astype(jnp.float32)
        row = lax.broadcasted_iota(jnp.int32, (UNIT_ROWS, HEAD_WIDTH), 0)
        position = jnp.right_shift(row, 1) + (counts[slot] - 1) * BLOCK_TOKENS
        own = jnp.where(jnp.bitwise_and(row, 1) == 0, token[0:1], token[1:2])
        last = starts[slot] + counts[slot] - 1
        held = units[last].astype(jnp.float32)
        kept = jnp.where(position < length, held, jnp.where(position == length, own, 0.0))
        units[last] = kept.astype(jnp.bfloat16)


def prepare(tables, pool, token, query, second_token, down, up):
    blocks, lengths, moving, _, buckets = tables
    return pl.pallas_call(
        prepare_kernel,
        out_shape=(
            jax.ShapeDtypeStruct((MOVING_REQUESTS, 16, HEAD_WIDTH), jnp.bfloat16),
            jax.ShapeDtypeStruct((FIRST_UNITS, UNIT_ROWS, HEAD_WIDTH), jnp.bfloat16),
            jax.ShapeDtypeStruct((MOST_UNITS - FIRST_UNITS, UNIT_ROWS, HEAD_WIDTH), jnp.bfloat16),
        ),
        in_specs=[ANY] * 10,
        out_specs=(VMEM, VMEM, VMEM),
        scratch_shapes=[
            pltpu.SMEM(lengths.shape, jnp.int32),
            pltpu.SMEM(moving.shape, jnp.int32),
            pltpu.SMEM(buckets.shape, jnp.int32),
            pltpu.SMEM(blocks.shape, jnp.int32),
            pltpu.VMEM(token.shape, jnp.bfloat16),
            pltpu.VMEM(query.shape, jnp.bfloat16),
            pltpu.VMEM(second_token.shape, jnp.bfloat16),
            pltpu.VMEM(down.shape, jnp.bfloat16),
            pltpu.VMEM(up.shape, jnp.bfloat16),
            pltpu.SemaphoreType.DMA((4,)),
            pltpu.SemaphoreType.DMA((5,)),
            pltpu.SemaphoreType.DMA((MOVING_REQUESTS, MAXB)),
        ],
        compiler_params=params(16),
        cost_estimate=cost(10**6, 3 * MIB),
        name="prepare",
    )(lengths, moving, buckets, blocks, pool, token, query, second_token, down, up)


def unpack_kernel(
    lengths_ref,
    moving_ref,
    buckets_ref,
    mask_ref,
    units,
    late_units,
    second_ref,
    rows_ref,
    second_out,
    cache_out,
    down_out,
    up_out,
    lengths,
    moving,
    buckets,
    mask,
    zeros,
    down,
    up,
    table_sems,
    block_sems,
    out_sems,
):
    tables = copies_of(
        [
            (lengths_ref, lengths),
            (moving_ref, moving),
            (buckets_ref, buckets),
            (mask_ref, mask),
        ],
        table_sems,
    )
    start_all(tables)
    zeros[...] = jnp.zeros_like(zeros)
    kept = second_ref[0:STAYING, :].astype(jnp.float32)
    came = rows_ref[...].astype(jnp.float32)
    second_out[...] = jnp.concatenate([kept, came], axis=0).astype(jnp.bfloat16)
    wait_all(tables)
    mate = jnp.bitwise_xor(lax.axis_index("replica"), mask[0])
    counts, starts, _ = unit_layout(mate, lengths, moving, buckets)

    def block_copy(slot, block, source):
        return pltpu.make_async_copy(
            source,
            cache_out.at[slot, pl.ds(block * BLOCK_ROWS, BLOCK_ROWS)],
            block_sems.at[slot, block],
        )

    for slot in range(MOVING_REQUESTS):
        for block in range(MAXB):
            pl.when(block < counts[slot])(
                lambda s=slot, b=block: block_copy(s, b, units.at[starts[s] + b]).start()
            )
            pl.when(block >= counts[slot])(lambda s=slot, b=block: block_copy(s, b, zeros).start())
    outs = []
    for slot in range(ADAPTER_COUNT):
        bucket = buckets[mate * ADAPTER_COUNT + slot]
        base = starts[MOVING_REQUESTS + slot]
        for kind in range(4):

            @pl.when(bucket == kind)
            def _(kind=kind, slot=slot, base=base):
                rows = UNIT_ROWS << kind
                lanes = RANK_UNIT << kind
                packed = jnp.concatenate(
                    [units[base + unit] for unit in range(1 << kind)], axis=0
                ).astype(jnp.float32)
                lane = lax.broadcasted_iota(jnp.int32, packed.shape, 1)
                for group in range(PADDED_RANK // lanes):
                    part = packed
                    if group:
                        part = pltpu.roll(part, PADDED_RANK - group * lanes, 1)
                    part = jnp.where(lane < lanes, part, 0.0).astype(jnp.bfloat16)
                    down[slot, group * rows : (group + 1) * rows, :] = part

        outs.append(pltpu.make_async_copy(down.at[slot], down_out.at[slot], out_sems.at[0, slot]))
        outs[-1].start()
        level = counts[MOVING_REQUESTS + slot]
        base = starts[MOVING_REQUESTS + ADAPTER_COUNT + slot]

        def up_unit(unit, carry, slot=slot, base=base, level=level):
            ranks = pl.ds(pl.multiple_of(unit * RANK_UNIT, RANK_UNIT), RANK_UNIT)
            place = base + jnp.minimum(unit, level - 1)
            held = jnp.where(
                place < FIRST_UNITS,
                units[jnp.minimum(place, FIRST_UNITS - 1)],
                late_units[jnp.maximum(place - FIRST_UNITS, 0)],
            )
            for column in range(UNIT_ROWS // RANK_UNIT):
                part = held[column * RANK_UNIT : (column + 1) * RANK_UNIT]
                up[slot, ranks, column * HEAD_WIDTH : (column + 1) * HEAD_WIDTH] = jnp.where(
                    unit < level, part, jnp.zeros_like(part)
                )
            return carry

        lax.fori_loop(0, ADAPTER_UNITS, up_unit, 0)
        outs.append(pltpu.make_async_copy(up.at[slot], up_out.at[slot], out_sems.at[1, slot]))
        outs[-1].start()
    for slot in range(MOVING_REQUESTS):
        for block in range(MAXB):
            block_copy(slot, block, zeros).wait()
    wait_all(outs)


def unpack(tables, mask, units, late_units, second, rows, down, up):
    _, lengths, moving, _, buckets = tables
    return pl.pallas_call(
        unpack_kernel,
        out_shape=(
            jax.ShapeDtypeStruct(second.shape, jnp.bfloat16),
            jax.ShapeDtypeStruct((MOVING_REQUESTS, CACHE_ROWS, HEAD_WIDTH), jnp.bfloat16),
            jax.ShapeDtypeStruct(down.shape, jnp.bfloat16),
            jax.ShapeDtypeStruct(up.shape, jnp.bfloat16),
        ),
        in_specs=[ANY] * 4 + [VMEM] * 4,
        out_specs=(VMEM,) + (ANY,) * 3,
        scratch_shapes=[
            pltpu.SMEM(lengths.shape, jnp.int32),
            pltpu.SMEM(moving.shape, jnp.int32),
            pltpu.SMEM(buckets.shape, jnp.int32),
            pltpu.SMEM(mask.shape, jnp.int32),
            pltpu.VMEM((BLOCK_ROWS, HEAD_WIDTH), jnp.bfloat16),
            pltpu.VMEM(down.shape, jnp.bfloat16),
            pltpu.VMEM(up.shape, jnp.bfloat16),
            pltpu.SemaphoreType.DMA((4,)),
            pltpu.SemaphoreType.DMA((MOVING_REQUESTS, MAXB)),
            pltpu.SemaphoreType.DMA((2, ADAPTER_COUNT)),
        ],
        compiler_params=params(16),
        cost_estimate=cost(10**6, 3 * MIB),
        name="unpack",
    )(lengths, moving, buckets, mask, units, late_units, second, rows)


def attend_kernel(
    arrived_ref,
    lengths_ref,
    moving_ref,
    buckets_ref,
    picks_ref,
    blocks_ref,
    pool_ref,
    query_ref,
    token_ref,
    second_query_ref,
    second_token_ref,
    down_ref,
    up_ref,
    weight_ref,
    shares_out,
    picks_out,
    up_out,
    more_out,
    lengths,
    moving,
    buckets,
    picks,
    blocks,
    raw_query,
    raw_token,
    raw_second_query,
    raw_second_token,
    down,
    pool,
    weight,
    queries,
    second_queries,
    tokens,
    second_tokens,
    attended,
    scores,
    pick_rows,
    table_sems,
    sems,
    pool_sems,
    weight_sems,
):
    replica = lax.axis_index("replica")
    parts = shares_out.shape[0]
    width = weight_ref.shape[1] // parts
    pool_parts = pool_sems.shape[0]
    per_part = pool_ref.shape[0] // pool_parts

    def pool_copy(part):
        where = pl.ds(part * per_part, per_part)
        return pltpu.make_async_copy(pool_ref.at[where], pool.at[where], pool_sems.at[part])

    def weight_copy(part):
        columns = pl.ds(pl.multiple_of(part * width, width), width)
        return pltpu.make_async_copy(
            weight_ref.at[:, columns], weight.at[part], weight_sems.at[part]
        )

    tables = copies_of(
        [
            (lengths_ref, lengths),
            (moving_ref, moving),
            (buckets_ref, buckets),
            (picks_ref, picks),
            (blocks_ref, blocks),
        ],
        table_sems,
    )
    arrays = copies_of(
        [
            (query_ref, raw_query),
            (token_ref, raw_token),
            (second_query_ref, raw_second_query),
            (second_token_ref, raw_second_token),
            (down_ref, down),
            (up_ref, up_out),
        ],
        sems,
    )
    start_all(tables)
    start_all(arrays[:4])
    for part in range(pool_parts):
        pool_copy(part).start()
    wait_all(arrays[:4])
    for h in range(GROUP):
        columns = slice(h * HEAD_WIDTH, (h + 1) * HEAD_WIDTH)
        rows = pl.ds(h, REQUEST_COUNT, stride=GROUP)
        queries[rows, :] = raw_query[:, columns].astype(jnp.float32)
        second_queries[rows, :] = raw_second_query[:, columns].astype(jnp.float32)
    tokens[:, 0:2, :] = raw_token[...].astype(jnp.float32)
    second_tokens[:, 0:2, :] = raw_second_token[...].astype(jnp.float32)
    for slot in range(MOVING_REQUESTS):
        row = STAYING + slot
        arrived = arrived_ref[slot].astype(jnp.float32)
        second_queries[row * GROUP : (row + 1) * GROUP, :] = arrived[0:GROUP]
        second_tokens[row, 0:2, :] = arrived[GROUP : GROUP + 2]
    wait_all(tables)

    def largest(other, most):
        return jnp.maximum(most, unit_layout(other, lengths, moving, buckets)[2])

    replicas = lengths_ref.shape[0] // REQUEST_COUNT
    most = lax.fori_loop(0, replicas, largest, jnp.int32(0))
    more_out[0] = (most > FIRST_UNITS).astype(jnp.int32)
    for part in range(pool_parts):
        pool_copy(part).wait()
    for part in range(parts):
        weight_copy(part).start()
    start_all(arrays[4:])

    leaving = [moving[replica * MOVING_REQUESTS + slot] for slot in range(MOVING_REQUESTS)]
    lane = lax.broadcasted_iota(jnp.int32, (2 * GROUP, CACHE_ROWS), 1)
    position = jnp.right_shift(lane, 1)
    is_key = jnp.bitwise_and(lane, 1) == 0
    second_half = lax.broadcasted_iota(jnp.int32, (2 * GROUP, 1), 0) >= GROUP

    scale = HEAD_WIDTH ** (-0.5)

    def second_row_of(request):
        second_row = request
        for slot in range(MOVING_REQUESTS):
            second_row = second_row - (leaving[slot] < request).astype(jnp.int32)
        for slot in range(MOVING_REQUESTS):
            second_row = jnp.where(leaving[slot] == request, STAYING + slot, second_row)
        return second_row

    def rows_of(row):
        return pl.ds(pl.multiple_of(row * GROUP, GROUP), GROUP)

    def held_of(request):
        return jnp.concatenate([pool[blocks[b, replica * REQUEST_COUNT + request]] for b in range(MAXB)], axis=0)

    def score_request(request):
        second_row = second_row_of(request)
        query = jnp.concatenate(
            [queries[rows_of(request), :], second_queries[rows_of(second_row), :]], axis=0
        )
        length = lengths[replica * REQUEST_COUNT + request]
        dots = lax.dot_general(
            query.astype(jnp.bfloat16),
            held_of(request),
            (((1,), (1,)), ((), ())),
            preferred_element_type=jnp.float32,
        )
        scores[request] = jnp.where(is_key & (position < length), dots * scale, -jnp.inf)

    def blend_request(request):
        second_row = second_row_of(request)
        query = jnp.concatenate(
            [queries[rows_of(request), :], second_queries[rows_of(second_row), :]], axis=0
        )
        pick = picks[replica * REQUEST_COUNT + request].astype(jnp.float32)
        pick_rows[pl.ds(request, 1), :] = jnp.full((1, HEAD_WIDTH), pick, jnp.float32)
        pick_rows[pl.ds(REQUEST_COUNT + second_row, 1), :] = jnp.full(
            (1, HEAD_WIDTH), pick, jnp.float32
        )
        token = tokens[request]
        own = second_tokens[second_row]
        score = scores[request]
        token_score = jnp.sum(query * token[0:1], axis=1, keepdims=True) * scale
        own_score = jnp.sum(query * own[0:1], axis=1, keepdims=True) * scale
        own_score = jnp.where(second_half, own_score, -jnp.inf)
        row_max = jnp.max(score, axis=1, keepdims=True)
        row_max = jnp.maximum(row_max, jnp.maximum(token_score, own_score))
        weights = jnp.exp(score - row_max)
        token_weight = jnp.exp(token_score - row_max)
        own_weight = jnp.exp(own_score - row_max)
        row_sum = jnp.sum(weights, axis=1, keepdims=True) + token_weight + own_weight
        weights = pltpu.roll(weights / row_sum, 1, 1).astype(jnp.bfloat16)
        token_weight = (token_weight / row_sum).astype(jnp.bfloat16).astype(jnp.float32)
        own_weight = (own_weight / row_sum).astype(jnp.bfloat16).astype(jnp.float32)
        blended = jnp.dot(weights, held_of(request), preferred_element_type=jnp.float32)
        blended = blended + token_weight * token[1:2] + own_weight * own[1:2]
        attended[rows_of(request), :] = blended[0:GROUP]
        attended[rows_of(REQUEST_COUNT + second_row), :] = blended[GROUP : 2 * GROUP]

    unrolled = 8

    def for_requests(work):
        def some_requests(step, carry):
            for k in range(unrolled):
                work(step * unrolled + k)
            return carry

        lax.fori_loop(0, REQUEST_COUNT // unrolled, some_requests, 0)

    for_requests(score_request)
    for_requests(blend_request)

    rows = 2 * REQUEST_COUNT
    held = jnp.concatenate(
        [attended[pl.ds(h, rows, stride=GROUP), :] for h in range(GROUP)], axis=1
    ).astype(jnp.bfloat16)
    pick_all = pick_rows[...]
    picks_out[...] = pick_all
    wait_all(arrays[4:])
    low = jnp.zeros((rows, PADDED_RANK), jnp.float32)
    lane = lax.broadcasted_iota(jnp.int32, (rows, PADDED_RANK), 1)
    for slot in range(ADAPTER_COUNT):
        level = jnp.left_shift(jnp.int32(1), buckets[replica * ADAPTER_COUNT + slot])
        scale = 2.0 / level.astype(jnp.float32)
        part = jnp.dot(held, down[slot], preferred_element_type=jnp.float32)
        live = (pick_all == slot) & (lane < RANK_UNIT * level)
        low = jnp.where(live, part * scale, low)
    low = low.astype(jnp.bfloat16)

    def one_part(part, carry):
        weight_copy(part).wait()
        share = jnp.dot(held, weight[part], preferred_element_type=jnp.float32)
        shares_out[part, :, 0:width] = share.astype(jnp.bfloat16)
        shares_out[part, :, width:] = low
        return carry

    lax.fori_loop(0, parts, one_part, 0)


def attend(tables, pool, weight, query, token, second_query, second_token, arrived, down, up, parts):
    blocks, lengths, moving, picks, buckets = tables
    rows = 2 * REQUEST_COUNT
    width = weight.shape[1] // parts
    depth = weight.shape[0]
    return pl.pallas_call(
        attend_kernel,
        out_shape=(
            jax.ShapeDtypeStruct((parts, rows, width + PADDED_RANK), jnp.bfloat16),
            jax.ShapeDtypeStruct((rows, PADDED_RANK), jnp.float32),
            jax.ShapeDtypeStruct(up.shape, jnp.bfloat16),
            jax.ShapeDtypeStruct((1,), jnp.int32),
        ),
        in_specs=[VMEM] + [ANY] * 13,
        out_specs=(VMEM,) * 3 + (SMEM,),
        scratch_shapes=[
            pltpu.SMEM(lengths.shape, jnp.int32),
            pltpu.SMEM(moving.shape, jnp.int32),
            pltpu.SMEM(buckets.shape, jnp.int32),
            pltpu.SMEM(picks.shape, jnp.int32),
            pltpu.SMEM(blocks.shape, jnp.int32),
            pltpu.VMEM(query.shape, jnp.bfloat16),
            pltpu.VMEM(token.shape, jnp.bfloat16),
            pltpu.VMEM(second_query.shape, jnp.bfloat16),
            pltpu.VMEM(second_token.shape, jnp.bfloat16),
            pltpu.VMEM(down.shape, jnp.bfloat16),
            pltpu.VMEM(pool.shape, jnp.bfloat16),
            pltpu.VMEM((parts, depth, width), jnp.bfloat16),
            pltpu.VMEM((REQUEST_COUNT * GROUP, HEAD_WIDTH), jnp.float32),
            pltpu.VMEM((REQUEST_COUNT * GROUP, HEAD_WIDTH), jnp.float32),
            pltpu.VMEM((REQUEST_COUNT, 8, HEAD_WIDTH), jnp.float32),
            pltpu.VMEM((REQUEST_COUNT, 8, HEAD_WIDTH), jnp.float32),
            pltpu.VMEM((rows * GROUP, HEAD_WIDTH), jnp.float32),
            pltpu.VMEM((REQUEST_COUNT, 2 * GROUP, CACHE_ROWS), jnp.float32),
            pltpu.VMEM((rows, HEAD_WIDTH), jnp.float32),
            pltpu.SemaphoreType.DMA((5,)),
            pltpu.SemaphoreType.DMA((6,)),
            pltpu.SemaphoreType.DMA((4,)),
            pltpu.SemaphoreType.DMA((parts,)),
        ],
        compiler_params=params(40),
        cost_estimate=cost(10**6, MIB),
        name="attend_project",
    )(
        arrived,
        lengths,
        moving,
        buckets,
        picks,
        blocks,
        pool,
        query,
        token,
        second_query,
        second_token,
        down,
        up,
        weight,
    )


def merge_kernel(shares_ref, send_out, keep_out):
    parts, near, _, _ = shares_ref.shape
    own = jnp.bitwise_and(lax.axis_index("tensor"), near - 1)

    def total(place):
        held = shares_ref[0, place].astype(jnp.float32)
        for part in range(1, parts):
            held = held + shares_ref[part, place].astype(jnp.float32)
        return held

    keep_out[...] = total(own)
    send_out[...] = total(near - 1 - own).astype(jnp.bfloat16)


def merge(shares):
    return pl.pallas_call(
        merge_kernel,
        out_shape=(
            jax.ShapeDtypeStruct(shares.shape[2:], jnp.bfloat16),
            jax.ShapeDtypeStruct(shares.shape[2:], jnp.float32),
        ),
        in_specs=[VMEM],
        out_specs=(VMEM,) * 2,
        compiler_params=params(16),
        cost_estimate=cost(10**6, MIB),
        name="merge",
    )(shares)


def finish_kernel(*refs):
    *shares, picks_ref, up_ref, first_out, second_out, leaving_out = refs
    rows = picks_ref.shape[0]
    width = first_out.shape[1]
    total = jnp.zeros((rows, width + PADDED_RANK), jnp.float32)
    for share in shares:
        pieces = [share[part] for part in range(share.shape[0])] if share.ndim == 3 else [share[...]]
        for piece in pieces:
            total = total + piece.astype(jnp.float32)
    base, low = total[:, 0:width], total[:, width:]
    picks = picks_ref[...]
    for slot in range(ADAPTER_COUNT):
        rest = jnp.where(picks == slot, low, 0.0)
        pieces = []
        for _ in range(3):
            piece = rest.astype(jnp.bfloat16)
            rest = rest - piece.astype(jnp.float32)
            pieces.append(piece)
        stacked = jnp.concatenate(pieces, axis=0)
        part = jnp.dot(stacked, up_ref[slot], preferred_element_type=jnp.float32)
        base = base + (part[0:rows] + part[rows : 2 * rows] + part[2 * rows : 3 * rows])
    result = base.astype(jnp.bfloat16)
    first_out[...] = result[0:REQUEST_COUNT]
    second_out[...] = result[REQUEST_COUNT:]
    leaving_out[...] = base[REQUEST_COUNT + STAYING :].astype(jnp.bfloat16)


def finish(shares, picks, up):
    width = shares[0].shape[-1] - PADDED_RANK
    return pl.pallas_call(
        finish_kernel,
        out_shape=(
            jax.ShapeDtypeStruct((REQUEST_COUNT, width), jnp.bfloat16),
            jax.ShapeDtypeStruct((REQUEST_COUNT, width), jnp.bfloat16),
            jax.ShapeDtypeStruct((MOVING_REQUESTS, width), jnp.bfloat16),
        ),
        in_specs=[VMEM] * (len(shares) + 2),
        out_specs=(VMEM,) * 3,
        compiler_params=params(16),
        cost_estimate=cost(10**6, MIB),
        name="finish",
    )(*shares, picks, up)


def swapped(mask):
    pairs = [(source, source ^ mask) for source in range(lax.axis_size("replica"))]
    return functools.partial(lax.ppermute, axis_name="replica", perm=pairs)


def sum_along_y(shares):
    parts, near = shares.shape[0], 2
    shares = shares.reshape(parts // near, near, *shares.shape[1:])
    groups = [list(range(start, parts, near)) for start in range(near)]
    shares = lax.all_to_all(shares, "tensor", 0, 0, tiled=True, axis_index_groups=groups)
    send, kept = merge(shares)
    pairs = [(source, source ^ 1) for source in range(parts)]
    return lax.ppermute(send, "tensor", pairs), kept


def branch(mask, tables, pool, weight, arrays, factors, moved_query, payload):
    query, token, second_query, second_token = arrays
    swap = swapped(mask) if mask else lambda value: value
    arrived = swap(moved_query)
    payload, arrived = lax.optimization_barrier((payload, arrived))
    units = swap(payload)
    shares, picks, held_up, more = attend(
        tables,
        pool,
        weight,
        query,
        token,
        second_query,
        second_token,
        arrived,
        *factors,
        lax.axis_size("tensor"),
    )
    if mask >= lax.axis_size("replica") // 2:
        shares = sum_along_y(shares)
    else:
        shares = (lax.all_to_all(shares, "tensor", 0, 0, tiled=True),)
    first, second, leaving = finish(shares, picks, held_up)
    return first, second, swap(leaving), units, more


def late_branch(mask, payload):
    return swapped(mask)(payload)


def keep(values):
    return values


def other_core(values):
    return tuple(swapped(1)(value) for value in values)


def shards(
    first_queries,
    first_key_value,
    second_queries,
    second_key_value,
    key_value_pool,
    request_blocks,
    lengths,
    moving_request_list,
    adapter_index,
    adapter_rank_bucket,
    replica_pair_mask,
    adapter_down_factors,
    adapter_up_factors,
    output_weight,
):
    tables = (
        request_blocks.T,
        lengths,
        moving_request_list,
        adapter_index,
        adapter_rank_bucket,
    )
    pool = key_value_pool.reshape(key_value_pool.shape[0], BLOCK_ROWS, HEAD_WIDTH)
    factors = (adapter_down_factors, adapter_up_factors)
    moved_query, payload, late_payload = prepare(
        tables,
        pool,
        first_key_value,
        second_queries,
        second_key_value,
        *factors,
    )
    mask = replica_pair_mask[0]
    to_other_core = jnp.bitwise_and(mask, 1) == 1
    moved_query = lax.cond(to_other_core, swapped(1), lambda value: value, moved_query)
    arrays = (first_queries, first_key_value, second_queries, second_key_value)
    branches = [
        functools.partial(branch, mask) for mask in range(0, lax.axis_size("replica"), 2)
    ]
    first, second, rows, units, more = lax.switch(
        jnp.right_shift(mask, 1), branches, tables, pool, output_weight, arrays, factors, moved_query, payload
    )
    units, rows = lax.cond(to_other_core, other_core, keep, (units, rows))
    late_branches = [
        functools.partial(late_branch, mask) for mask in range(1, lax.axis_size("replica"))
    ]
    late_units = lax.cond(
        more[0] == 1,
        lambda value: lax.switch(mask - 1, late_branches, value),
        keep,
        late_payload,
    )
    second, cache, down, up = unpack(
        tables, replica_pair_mask, units, late_units, second, rows, *factors
    )
    cache = cache.reshape(MOVING_REQUESTS, MAXB * BLOCK_TOKENS, 2, HEAD_WIDTH)
    return first, second, cache, down, up


def solution(mesh):
    placed = (
        P("replica", "tensor"),
        P("replica", None, "tensor"),
        P("replica", "tensor"),
        P("replica", None, "tensor"),
        P("replica", None, None, "tensor"),
        P(),
        P(),
        P(),
        P(),
        P(),
        P(),
        P("replica", "tensor", None),
        P("replica", None, "tensor"),
        P("tensor", None),
    )
    return jax.shard_map(
        shards,
        mesh=mesh,
        in_specs=placed,
        out_specs=(
            P("replica", "tensor"),
            P("replica", "tensor"),
            P("replica", None, None, "tensor"),
            P("replica", "tensor", None),
            P("replica", None, "tensor"),
        ),
        check_vma=False,
    )
```

```python
import functools

import jax
import jax.numpy as jnp
from jax import lax
from jax.experimental import pallas as pl
from jax.experimental.pallas import tpu as pltpu
from jax.sharding import PartitionSpec as P

HEAD_WIDTH = 128
GROUP = 8
PADDED_RANK = 128
REQUEST_COUNT = 16
MOVING_REQUESTS = 2
STAYING = REQUEST_COUNT - MOVING_REQUESTS
ADAPTER_COUNT = 2
BLOCK_TOKENS = 64
BLOCK_ROWS = 2 * BLOCK_TOKENS
MAXB = 8
CACHE_ROWS = MAXB * BLOCK_ROWS
MIB = 1 << 20

UNIT_ROWS = 128
RANK_UNIT = 16
ADAPTER_UNITS = PADDED_RANK // RANK_UNIT
MOST_UNITS = MOVING_REQUESTS * MAXB + 2 * ADAPTER_COUNT * ADAPTER_UNITS
FIRST_UNITS = 40

ANY = pl.BlockSpec(memory_space=pl.ANY)
VMEM = pl.BlockSpec(memory_space=pltpu.VMEM)
SMEM = pl.BlockSpec(memory_space=pltpu.SMEM)


def params(mib):
    return pltpu.CompilerParams(vmem_limit_bytes=mib * MIB)


def cost(flops, moved):
    return pl.CostEstimate(flops=flops, bytes_accessed=moved, transcendentals=0)


def copies_of(pairs, sems):
    return [
        pltpu.make_async_copy(source, target, sems.at[place])
        for place, (source, target) in enumerate(pairs)
    ]


def start_all(copies):
    for copy in copies:
        copy.start()


def wait_all(copies):
    for copy in copies:
        copy.wait()


def unit_layout(replica, lengths, moving, buckets):
    counts = []
    for slot in range(MOVING_REQUESTS):
        request = moving[replica * MOVING_REQUESTS + slot]
        length = lengths[replica * REQUEST_COUNT + request]
        counts.append(lax.div(length, BLOCK_TOKENS) + 1)
    levels = [
        jnp.left_shift(jnp.int32(1), buckets[replica * ADAPTER_COUNT + slot])
        for slot in range(ADAPTER_COUNT)
    ]
    counts = counts + levels + levels
    starts, total = [], jnp.int32(0)
    for count in counts:
        starts.append(total)
        total = total + count
    return counts, starts, total


def pack_down(source, bucket):
    rows = UNIT_ROWS << bucket
    lanes = RANK_UNIT << bucket
    lane = lax.broadcasted_iota(jnp.int32, (rows, PADDED_RANK), 1)
    packed = jnp.zeros((rows, PADDED_RANK), jnp.float32)
    for group in range(PADDED_RANK // lanes):
        part = source[group * rows : (group + 1) * rows, :].astype(jnp.float32)
        if group:
            part = pltpu.roll(part, group * lanes, 1)
        here = (lane >= group * lanes) & (lane < (group + 1) * lanes)
        packed = jnp.where(here, part, packed)
    return packed.astype(jnp.bfloat16)


def prepare_kernel(
    lengths_ref,
    moving_ref,
    buckets_ref,
    blocks_ref,
    pool_ref,
    token_ref,
    query_ref,
    second_token_ref,
    down_ref,
    up_ref,
    query_out,
    units,
    late_units,
    lengths,
    moving,
    buckets,
    blocks,
    tokens,
    queries,
    second_tokens,
    down,
    up,
    table_sems,
    sems,
    block_sems,
):
    replica = lax.axis_index("replica")
    tables = copies_of(
        [
            (lengths_ref, lengths),
            (moving_ref, moving),
            (buckets_ref, buckets),
            (blocks_ref, blocks),
        ],
        table_sems,
    )
    arrays = copies_of(
        [
            (query_ref, queries),
            (second_token_ref, second_tokens),
            (token_ref, tokens),
            (down_ref, down),
            (up_ref, up),
        ],
        sems,
    )
    start_all(tables)
    start_all(arrays)
    wait_all(tables)
    counts, starts, _ = unit_layout(replica, lengths, moving, buckets)
    requests = [moving[replica * MOVING_REQUESTS + slot] for slot in range(MOVING_REQUESTS)]

    def block_copy(slot, block):
        return pltpu.make_async_copy(
            pool_ref.at[blocks[block, replica * REQUEST_COUNT + requests[slot]]],
            units.at[starts[slot] + block],
            block_sems.at[slot, block],
        )

    for slot in range(MOVING_REQUESTS):
        for block in range(MAXB):
            pl.when(block < counts[slot])(lambda s=slot, b=block: block_copy(s, b).start())

    wait_all(arrays[:3])
    for slot in range(MOVING_REQUESTS):
        row = STAYING + slot
        heads = [
            queries[row : row + 1, h * HEAD_WIDTH : (h + 1) * HEAD_WIDTH].astype(jnp.float32)
            for h in range(GROUP)
        ]
        own = second_tokens[row].astype(jnp.float32)
        padding = jnp.zeros((16 - GROUP - 2, HEAD_WIDTH), jnp.float32)
        query_out[slot] = jnp.concatenate(heads + [own, padding], axis=0).astype(jnp.bfloat16)
    wait_all(arrays[3:])
    for slot in range(ADAPTER_COUNT):
        bucket = buckets[replica * ADAPTER_COUNT + slot]
        level = jnp.left_shift(jnp.int32(1), bucket)
        scale = 2.0 / level.astype(jnp.float32)
        base = starts[MOVING_REQUESTS + slot]
        for kind in range(4):

            @pl.when(bucket == kind)
            def _(kind=kind, slot=slot, base=base):
                packed = pack_down(down.at[slot], kind)
                for unit in range(1 << kind):
                    units[base + unit] = packed[unit * UNIT_ROWS : (unit + 1) * UNIT_ROWS]

        base = starts[MOVING_REQUESTS + ADAPTER_COUNT + slot]

        def up_unit(unit, carry, slot=slot, base=base, scale=scale):
            ranks = pl.ds(pl.multiple_of(unit * RANK_UNIT, RANK_UNIT), RANK_UNIT)
            part = (up[slot, ranks, :].astype(jnp.float32) * scale).astype(jnp.bfloat16)
            place = base + unit

            def put(target, where):
                for column in range(UNIT_ROWS // RANK_UNIT):
                    target[where, column * RANK_UNIT : (column + 1) * RANK_UNIT, :] = part[
                        :, column * HEAD_WIDTH : (column + 1) * HEAD_WIDTH
                    ]

            pl.when(place < FIRST_UNITS)(lambda: put(units, place))
            pl.when(place >= FIRST_UNITS)(lambda: put(late_units, place - FIRST_UNITS))
            return carry

        lax.fori_loop(0, level, up_unit, 0)
    for slot in range(MOVING_REQUESTS):
        for block in range(MAXB):
            pl.when(block < counts[slot])(lambda s=slot, b=block: block_copy(s, b).wait())
        length = lengths[replica * REQUEST_COUNT + requests[slot]]
        token = tokens[requests[slot]].astype(jnp.float32)
        row = lax.broadcasted_iota(jnp.int32, (UNIT_ROWS, HEAD_WIDTH), 0)
        position = jnp.right_shift(row, 1) + (counts[slot] - 1) * BLOCK_TOKENS
        own = jnp.where(jnp.bitwise_and(row, 1) == 0, token[0:1], token[1:2])
        last = starts[slot] + counts[slot] - 1
        held = units[last].astype(jnp.float32)
        kept = jnp.where(position < length, held, jnp.where(position == length, own, 0.0))
        units[last] = kept.astype(jnp.bfloat16)


def prepare(tables, pool, token, query, second_token, down, up):
    blocks, lengths, moving, _, buckets = tables
    return pl.pallas_call(
        prepare_kernel,
        out_shape=(
            jax.ShapeDtypeStruct((MOVING_REQUESTS, 16, HEAD_WIDTH), jnp.bfloat16),
            jax.ShapeDtypeStruct((FIRST_UNITS, UNIT_ROWS, HEAD_WIDTH), jnp.bfloat16),
            jax.ShapeDtypeStruct((MOST_UNITS - FIRST_UNITS, UNIT_ROWS, HEAD_WIDTH), jnp.bfloat16),
        ),
        in_specs=[ANY] * 10,
        out_specs=(VMEM, VMEM, VMEM),
        scratch_shapes=[
            pltpu.SMEM(lengths.shape, jnp.int32),
            pltpu.SMEM(moving.shape, jnp.int32),
            pltpu.SMEM(buckets.shape, jnp.int32),
            pltpu.SMEM(blocks.shape, jnp.int32),
            pltpu.VMEM(token.shape, jnp.bfloat16),
            pltpu.VMEM(query.shape, jnp.bfloat16),
            pltpu.VMEM(second_token.shape, jnp.bfloat16),
            pltpu.VMEM(down.shape, jnp.bfloat16),
            pltpu.VMEM(up.shape, jnp.bfloat16),
            pltpu.SemaphoreType.DMA((4,)),
            pltpu.SemaphoreType.DMA((5,)),
            pltpu.SemaphoreType.DMA((MOVING_REQUESTS, MAXB)),
        ],
        compiler_params=params(16),
        cost_estimate=cost(10**6, 3 * MIB),
        name="prepare",
    )(lengths, moving, buckets, blocks, pool, token, query, second_token, down, up)


def unpack_kernel(
    lengths_ref,
    moving_ref,
    buckets_ref,
    mask_ref,
    units,
    late_units,
    cache_out,
    down_out,
    up_out,
    lengths,
    moving,
    buckets,
    mask,
    zeros,
    down,
    up,
    table_sems,
    block_sems,
    out_sems,
):
    tables = copies_of(
        [
            (lengths_ref, lengths),
            (moving_ref, moving),
            (buckets_ref, buckets),
            (mask_ref, mask),
        ],
        table_sems,
    )
    start_all(tables)
    zeros[...] = jnp.zeros_like(zeros)
    wait_all(tables)
    mate = jnp.bitwise_xor(lax.axis_index("replica"), mask[0])
    counts, starts, _ = unit_layout(mate, lengths, moving, buckets)

    def block_copy(slot, block, source):
        return pltpu.make_async_copy(
            source,
            cache_out.at[slot, pl.ds(block * BLOCK_ROWS, BLOCK_ROWS)],
            block_sems.at[slot, block],
        )

    def pick(values, slot):
        return jnp.where(slot == 0, values[0], values[1])

    def start_blocks(place, carry):
        slot, block = lax.div(place, MAXB), lax.rem(place, MAXB)
        held = block < pick(counts[:2], slot)
        source = pick(starts[:2], slot) + block
        pl.when(held)(lambda: block_copy(slot, block, units.at[source]).start())
        pl.when(jnp.logical_not(held))(lambda: block_copy(slot, block, zeros).start())
        return carry

    def wait_blocks(place, carry):
        block_copy(lax.div(place, MAXB), lax.rem(place, MAXB), zeros).wait()
        return carry

    def factor_copies(slot):
        return (
            pltpu.make_async_copy(down.at[slot], down_out.at[slot], out_sems.at[0, slot]),
            pltpu.make_async_copy(up.at[slot], up_out.at[slot], out_sems.at[1, slot]),
        )

    lax.fori_loop(0, MOVING_REQUESTS * MAXB, start_blocks, 0)

    def factors(slot, carry):
        bucket = buckets[mate * ADAPTER_COUNT + slot]
        base = pick(starts[2:4], slot)
        for kind in range(4):

            @pl.when(bucket == kind)
            def _(kind=kind):
                rows = UNIT_ROWS << kind
                lanes = RANK_UNIT << kind
                packed = jnp.concatenate(
                    [units[base + unit] for unit in range(1 << kind)], axis=0
                ).astype(jnp.float32)
                lane = lax.broadcasted_iota(jnp.int32, packed.shape, 1)
                for group in range(PADDED_RANK // lanes):
                    part = packed
                    if group:
                        part = pltpu.roll(part, PADDED_RANK - group * lanes, 1)
                    part = jnp.where(lane < lanes, part, 0.0).astype(jnp.bfloat16)
                    down[slot, group * rows : (group + 1) * rows, :] = part

        copy_down, copy_up = factor_copies(slot)
        copy_down.start()
        level = jnp.left_shift(jnp.int32(1), bucket)
        up_base = pick(starts[4:6], slot)

        def up_unit(unit, carry):
            ranks = pl.ds(pl.multiple_of(unit * RANK_UNIT, RANK_UNIT), RANK_UNIT)
            place = up_base + jnp.minimum(unit, level - 1)
            held = jnp.where(
                place < FIRST_UNITS,
                units[jnp.minimum(place, FIRST_UNITS - 1)],
                late_units[jnp.maximum(place - FIRST_UNITS, 0)],
            )
            for column in range(UNIT_ROWS // RANK_UNIT):
                part = held[column * RANK_UNIT : (column + 1) * RANK_UNIT]
                up[slot, ranks, column * HEAD_WIDTH : (column + 1) * HEAD_WIDTH] = jnp.where(
                    unit < level, part, jnp.zeros_like(part)
                )
            return carry

        lax.fori_loop(0, ADAPTER_UNITS, up_unit, 0)
        copy_up.start()
        return carry

    lax.fori_loop(0, ADAPTER_COUNT, factors, 0)
    lax.fori_loop(0, MOVING_REQUESTS * MAXB, wait_blocks, 0)
    for slot in range(ADAPTER_COUNT):
        wait_all(factor_copies(slot))


def unpack(tables, mask, units, late_units, down, up):
    _, lengths, moving, _, buckets = tables
    return pl.pallas_call(
        unpack_kernel,
        out_shape=(
            jax.ShapeDtypeStruct((MOVING_REQUESTS, CACHE_ROWS, HEAD_WIDTH), jnp.bfloat16),
            jax.ShapeDtypeStruct(down.shape, jnp.bfloat16),
            jax.ShapeDtypeStruct(up.shape, jnp.bfloat16),
        ),
        in_specs=[ANY] * 4 + [VMEM] * 2,
        out_specs=(ANY,) * 3,
        scratch_shapes=[
            pltpu.SMEM(lengths.shape, jnp.int32),
            pltpu.SMEM(moving.shape, jnp.int32),
            pltpu.SMEM(buckets.shape, jnp.int32),
            pltpu.SMEM(mask.shape, jnp.int32),
            pltpu.VMEM((BLOCK_ROWS, HEAD_WIDTH), jnp.bfloat16),
            pltpu.VMEM(down.shape, jnp.bfloat16),
            pltpu.VMEM(up.shape, jnp.bfloat16),
            pltpu.SemaphoreType.DMA((4,)),
            pltpu.SemaphoreType.DMA((MOVING_REQUESTS, MAXB)),
            pltpu.SemaphoreType.DMA((2, ADAPTER_COUNT)),
        ],
        compiler_params=params(16),
        cost_estimate=cost(10**6, 3 * MIB),
        name="unpack",
    )(lengths, moving, buckets, mask, units, late_units)


def attend_kernel(
    arrived_ref,
    lengths_ref,
    moving_ref,
    buckets_ref,
    picks_ref,
    blocks_ref,
    pool_ref,
    query_ref,
    token_ref,
    second_query_ref,
    second_token_ref,
    down_ref,
    up_ref,
    weight_ref,
    shares_out,
    picks_out,
    up_out,
    more_out,
    lengths,
    moving,
    buckets,
    picks,
    blocks,
    raw_query,
    raw_token,
    raw_second_query,
    raw_second_token,
    down,
    pool,
    weight,
    queries,
    second_queries,
    tokens,
    second_tokens,
    attended,
    scores,
    pick_rows,
    table_sems,
    sems,
    pool_sems,
    weight_sems,
):
    replica = lax.axis_index("replica")
    parts = shares_out.shape[0]
    width = weight_ref.shape[1] // parts
    pool_parts = pool_sems.shape[0]
    per_part = pool_ref.shape[0] // pool_parts

    def pool_copy(part):
        where = pl.ds(part * per_part, per_part)
        return pltpu.make_async_copy(pool_ref.at[where], pool.at[where], pool_sems.at[part])

    def weight_copy(part):
        columns = pl.ds(pl.multiple_of(part * width, width), width)
        return pltpu.make_async_copy(
            weight_ref.at[:, columns], weight.at[part], weight_sems.at[part]
        )

    tables = copies_of(
        [
            (lengths_ref, lengths),
            (moving_ref, moving),
            (buckets_ref, buckets),
            (picks_ref, picks),
            (blocks_ref, blocks),
        ],
        table_sems,
    )
    arrays = copies_of(
        [
            (query_ref, raw_query),
            (token_ref, raw_token),
            (second_query_ref, raw_second_query),
            (second_token_ref, raw_second_token),
            (down_ref, down),
            (up_ref, up_out),
        ],
        sems,
    )
    start_all(tables)
    start_all(arrays[:4])
    for part in range(pool_parts):
        pool_copy(part).start()
    wait_all(arrays[:4])
    for h in range(GROUP):
        columns = slice(h * HEAD_WIDTH, (h + 1) * HEAD_WIDTH)
        rows = pl.ds(h, REQUEST_COUNT, stride=GROUP)
        queries[rows, :] = raw_query[:, columns].astype(jnp.float32)
        second_queries[rows, :] = raw_second_query[:, columns].astype(jnp.float32)
    tokens[:, 0:2, :] = raw_token[...].astype(jnp.float32)
    second_tokens[:, 0:2, :] = raw_second_token[...].astype(jnp.float32)
    for slot in range(MOVING_REQUESTS):
        row = STAYING + slot
        arrived = arrived_ref[slot].astype(jnp.float32)
        second_queries[row * GROUP : (row + 1) * GROUP, :] = arrived[0:GROUP]
        second_tokens[row, 0:2, :] = arrived[GROUP : GROUP + 2]
    wait_all(tables)

    def largest(other, most):
        return jnp.maximum(most, unit_layout(other, lengths, moving, buckets)[2])

    replicas = lengths_ref.shape[0] // REQUEST_COUNT
    most = lax.fori_loop(0, replicas, largest, jnp.int32(0))
    more_out[0] = (most > FIRST_UNITS).astype(jnp.int32)
    for part in range(pool_parts):
        pool_copy(part).wait()
    for part in range(parts):
        weight_copy(part).start()
    start_all(arrays[4:])

    leaving = [moving[replica * MOVING_REQUESTS + slot] for slot in range(MOVING_REQUESTS)]
    lane = lax.broadcasted_iota(jnp.int32, (2 * GROUP, CACHE_ROWS), 1)
    position = jnp.right_shift(lane, 1)
    is_key = jnp.bitwise_and(lane, 1) == 0
    second_half = lax.broadcasted_iota(jnp.int32, (2 * GROUP, 1), 0) >= GROUP

    scale = HEAD_WIDTH ** (-0.5)

    def second_row_of(request):
        second_row = request
        for slot in range(MOVING_REQUESTS):
            second_row = second_row - (leaving[slot] < request).astype(jnp.int32)
        for slot in range(MOVING_REQUESTS):
            second_row = jnp.where(leaving[slot] == request, STAYING + slot, second_row)
        return second_row

    def rows_of(row):
        return pl.ds(pl.multiple_of(row * GROUP, GROUP), GROUP)

    def held_of(request):
        return jnp.concatenate([pool[blocks[b, replica * REQUEST_COUNT + request]] for b in range(MAXB)], axis=0)

    def score_request(request):
        second_row = second_row_of(request)
        query = jnp.concatenate(
            [queries[rows_of(request), :], second_queries[rows_of(second_row), :]], axis=0
        )
        length = lengths[replica * REQUEST_COUNT + request]
        dots = lax.dot_general(
            query.astype(jnp.bfloat16),
            held_of(request),
            (((1,), (1,)), ((), ())),
            preferred_element_type=jnp.float32,
        )
        scores[request] = jnp.where(is_key & (position < length), dots * scale, -jnp.inf)

    def blend_request(request):
        second_row = second_row_of(request)
        query = jnp.concatenate(
            [queries[rows_of(request), :], second_queries[rows_of(second_row), :]], axis=0
        )
        pick = picks[replica * REQUEST_COUNT + request].astype(jnp.float32)
        pick_rows[pl.ds(request, 1), :] = jnp.full((1, HEAD_WIDTH), pick, jnp.float32)
        pick_rows[pl.ds(REQUEST_COUNT + second_row, 1), :] = jnp.full(
            (1, HEAD_WIDTH), pick, jnp.float32
        )
        token = tokens[request]
        own = second_tokens[second_row]
        score = scores[request]
        token_score = jnp.sum(query * token[0:1], axis=1, keepdims=True) * scale
        own_score = jnp.sum(query * own[0:1], axis=1, keepdims=True) * scale
        own_score = jnp.where(second_half, own_score, -jnp.inf)
        row_max = jnp.max(score, axis=1, keepdims=True)
        row_max = jnp.maximum(row_max, jnp.maximum(token_score, own_score))
        weights = jnp.exp(score - row_max)
        token_weight = jnp.exp(token_score - row_max)
        own_weight = jnp.exp(own_score - row_max)
        row_sum = jnp.sum(weights, axis=1, keepdims=True) + token_weight + own_weight
        weights = pltpu.roll(weights / row_sum, 1, 1).astype(jnp.bfloat16)
        token_weight = (token_weight / row_sum).astype(jnp.bfloat16).astype(jnp.float32)
        own_weight = (own_weight / row_sum).astype(jnp.bfloat16).astype(jnp.float32)
        blended = jnp.dot(weights, held_of(request), preferred_element_type=jnp.float32)
        blended = blended + token_weight * token[1:2] + own_weight * own[1:2]
        attended[rows_of(request), :] = blended[0:GROUP]
        attended[rows_of(REQUEST_COUNT + second_row), :] = blended[GROUP : 2 * GROUP]

    unrolled = 4

    def for_requests(work):
        def some_requests(step, carry):
            for k in range(unrolled):
                work(step * unrolled + k)
            return carry

        lax.fori_loop(0, REQUEST_COUNT // unrolled, some_requests, 0)

    for_requests(score_request)
    for_requests(blend_request)

    rows = 2 * REQUEST_COUNT
    held = jnp.concatenate(
        [attended[pl.ds(h, rows, stride=GROUP), :] for h in range(GROUP)], axis=1
    ).astype(jnp.bfloat16)
    pick_all = pick_rows[...]
    picks_out[...] = pick_all
    wait_all(arrays[4:])
    low = jnp.zeros((rows, PADDED_RANK), jnp.float32)
    lane = lax.broadcasted_iota(jnp.int32, (rows, PADDED_RANK), 1)
    for slot in range(ADAPTER_COUNT):
        level = jnp.left_shift(jnp.int32(1), buckets[replica * ADAPTER_COUNT + slot])
        scale = 2.0 / level.astype(jnp.float32)
        part = jnp.dot(held, down[slot], preferred_element_type=jnp.float32)
        live = (pick_all == slot) & (lane < RANK_UNIT * level)
        low = jnp.where(live, part * scale, low)
    low = low.astype(jnp.bfloat16)

    def one_part(part, carry):
        weight_copy(part).wait()
        share = jnp.dot(held, weight[part], preferred_element_type=jnp.float32)
        shares_out[part, :, 0:width] = share.astype(jnp.bfloat16)
        shares_out[part, :, width:] = low
        return carry

    lax.fori_loop(0, parts, one_part, 0)


def attend(tables, pool, weight, query, token, second_query, second_token, arrived, down, up, parts):
    blocks, lengths, moving, picks, buckets = tables
    rows = 2 * REQUEST_COUNT
    width = weight.shape[1] // parts
    depth = weight.shape[0]
    return pl.pallas_call(
        attend_kernel,
        out_shape=(
            jax.ShapeDtypeStruct((parts, rows, width + PADDED_RANK), jnp.bfloat16),
            jax.ShapeDtypeStruct((rows, PADDED_RANK), jnp.float32),
            jax.ShapeDtypeStruct(up.shape, jnp.bfloat16),
            jax.ShapeDtypeStruct((1,), jnp.int32),
        ),
        in_specs=[VMEM] + [ANY] * 13,
        out_specs=(VMEM,) * 3 + (SMEM,),
        scratch_shapes=[
            pltpu.SMEM(lengths.shape, jnp.int32),
            pltpu.SMEM(moving.shape, jnp.int32),
            pltpu.SMEM(buckets.shape, jnp.int32),
            pltpu.SMEM(picks.shape, jnp.int32),
            pltpu.SMEM(blocks.shape, jnp.int32),
            pltpu.VMEM(query.shape, jnp.bfloat16),
            pltpu.VMEM(token.shape, jnp.bfloat16),
            pltpu.VMEM(second_query.shape, jnp.bfloat16),
            pltpu.VMEM(second_token.shape, jnp.bfloat16),
            pltpu.VMEM(down.shape, jnp.bfloat16),
            pltpu.VMEM(pool.shape, jnp.bfloat16),
            pltpu.VMEM((parts, depth, width), jnp.bfloat16),
            pltpu.VMEM((REQUEST_COUNT * GROUP, HEAD_WIDTH), jnp.float32),
            pltpu.VMEM((REQUEST_COUNT * GROUP, HEAD_WIDTH), jnp.float32),
            pltpu.VMEM((REQUEST_COUNT, 8, HEAD_WIDTH), jnp.float32),
            pltpu.VMEM((REQUEST_COUNT, 8, HEAD_WIDTH), jnp.float32),
            pltpu.VMEM((rows * GROUP, HEAD_WIDTH), jnp.float32),
            pltpu.VMEM((REQUEST_COUNT, 2 * GROUP, CACHE_ROWS), jnp.float32),
            pltpu.VMEM((rows, HEAD_WIDTH), jnp.float32),
            pltpu.SemaphoreType.DMA((5,)),
            pltpu.SemaphoreType.DMA((6,)),
            pltpu.SemaphoreType.DMA((4,)),
            pltpu.SemaphoreType.DMA((parts,)),
        ],
        compiler_params=params(40),
        cost_estimate=cost(10**6, MIB),
        name="attend_project",
    )(
        arrived,
        lengths,
        moving,
        buckets,
        picks,
        blocks,
        pool,
        query,
        token,
        second_query,
        second_token,
        down,
        up,
        weight,
    )


def merge_kernel(shares_ref, send_out, keep_out):
    parts, near, _, _ = shares_ref.shape
    own = jnp.bitwise_and(lax.axis_index("tensor"), near - 1)

    def total(place):
        held = shares_ref[0, place].astype(jnp.float32)
        for part in range(1, parts):
            held = held + shares_ref[part, place].astype(jnp.float32)
        return held

    keep_out[...] = total(own)
    send_out[...] = total(near - 1 - own).astype(jnp.bfloat16)


def merge(shares):
    return pl.pallas_call(
        merge_kernel,
        out_shape=(
            jax.ShapeDtypeStruct(shares.shape[2:], jnp.bfloat16),
            jax.ShapeDtypeStruct(shares.shape[2:], jnp.float32),
        ),
        in_specs=[VMEM],
        out_specs=(VMEM,) * 2,
        compiler_params=params(16),
        cost_estimate=cost(10**6, MIB),
        name="merge",
    )(shares)


def finish_kernel(*refs):
    *shares, picks_ref, up_ref, first_out, second_out, leaving_out = refs
    rows = picks_ref.shape[0]
    width = first_out.shape[1]
    total = jnp.zeros((rows, width + PADDED_RANK), jnp.float32)
    for share in shares:
        pieces = [share[part] for part in range(share.shape[0])] if share.ndim == 3 else [share[...]]
        for piece in pieces:
            total = total + piece.astype(jnp.float32)
    base, low = total[:, 0:width], total[:, width:]
    picks = picks_ref[...]
    for slot in range(ADAPTER_COUNT):
        rest = jnp.where(picks == slot, low, 0.0)
        pieces = []
        for _ in range(3):
            piece = rest.astype(jnp.bfloat16)
            rest = rest - piece.astype(jnp.float32)
            pieces.append(piece)
        stacked = jnp.concatenate(pieces, axis=0)
        part = jnp.dot(stacked, up_ref[slot], preferred_element_type=jnp.float32)
        base = base + (part[0:rows] + part[rows : 2 * rows] + part[2 * rows : 3 * rows])
    result = base.astype(jnp.bfloat16)
    first_out[...] = result[0:REQUEST_COUNT]
    second_out[...] = result[REQUEST_COUNT:]
    leaving_out[...] = base[REQUEST_COUNT + STAYING :].astype(jnp.bfloat16)


def finish(shares, picks, up):
    width = shares[0].shape[-1] - PADDED_RANK
    return pl.pallas_call(
        finish_kernel,
        out_shape=(
            jax.ShapeDtypeStruct((REQUEST_COUNT, width), jnp.bfloat16),
            jax.ShapeDtypeStruct((REQUEST_COUNT, width), jnp.bfloat16),
            jax.ShapeDtypeStruct((MOVING_REQUESTS, width), jnp.bfloat16),
        ),
        in_specs=[VMEM] * (len(shares) + 2),
        out_specs=(VMEM,) * 3,
        compiler_params=params(16),
        cost_estimate=cost(10**6, MIB),
        name="finish",
    )(*shares, picks, up)


def swapped(mask):
    pairs = [(source, source ^ mask) for source in range(lax.axis_size("replica"))]
    return functools.partial(lax.ppermute, axis_name="replica", perm=pairs)


def sum_along_y(shares):
    parts, near = shares.shape[0], 2
    shares = shares.reshape(parts // near, near, *shares.shape[1:])
    groups = [list(range(start, parts, near)) for start in range(near)]
    shares = lax.all_to_all(shares, "tensor", 0, 0, tiled=True, axis_index_groups=groups)
    send, kept = merge(shares)
    pairs = [(source, source ^ 1) for source in range(parts)]
    return lax.ppermute(send, "tensor", pairs), kept


def branch(mask, tables, pool, weight, arrays, factors, moved_query, payload):
    query, token, second_query, second_token = arrays
    swap = swapped(mask) if mask else lambda value: value
    arrived = swap(moved_query)
    payload, arrived = lax.optimization_barrier((payload, arrived))
    units = swap(payload)
    shares, picks, held_up, more = attend(
        tables,
        pool,
        weight,
        query,
        token,
        second_query,
        second_token,
        arrived,
        *factors,
        lax.axis_size("tensor"),
    )
    if mask >= lax.axis_size("replica") // 2:
        shares = sum_along_y(shares)
    else:
        shares = (lax.all_to_all(shares, "tensor", 0, 0, tiled=True),)
    first, second, leaving = finish(shares, picks, held_up)
    return first, second, leaving, units, more


def late_branch(mask, payload):
    return swapped(mask)(payload) if mask else payload


def last_branch(mask, tables, masks, units, late_units, second, leaving, factors):
    arrived = swapped(mask)(leaving)
    cache, down, up = unpack(tables, masks, units, late_units, *factors)
    return lax.dynamic_update_slice(second, arrived, (STAYING, 0)), cache, down, up


def keep(values):
    return values


def other_core(value):
    return swapped(1)(value)


def shards(
    first_queries,
    first_key_value,
    second_queries,
    second_key_value,
    key_value_pool,
    request_blocks,
    lengths,
    moving_request_list,
    adapter_index,
    adapter_rank_bucket,
    replica_pair_mask,
    adapter_down_factors,
    adapter_up_factors,
    output_weight,
):
    tables = (
        request_blocks.T,
        lengths,
        moving_request_list,
        adapter_index,
        adapter_rank_bucket,
    )
    pool = key_value_pool.reshape(key_value_pool.shape[0], BLOCK_ROWS, HEAD_WIDTH)
    factors = (adapter_down_factors, adapter_up_factors)
    moved_query, payload, late_payload = prepare(
        tables,
        pool,
        first_key_value,
        second_queries,
        second_key_value,
        *factors,
    )
    mask = replica_pair_mask[0]
    chip_mask = jnp.right_shift(mask, 1)
    to_other_core = jnp.bitwise_and(mask, 1) == 1
    moved_query = lax.cond(to_other_core, swapped(1), lambda value: value, moved_query)
    arrays = (first_queries, first_key_value, second_queries, second_key_value)
    branches = [
        functools.partial(branch, mask) for mask in range(0, lax.axis_size("replica"), 2)
    ]
    first, second, leaving, units, more = lax.switch(
        chip_mask, branches, tables, pool, output_weight, arrays, factors, moved_query, payload
    )
    units = lax.cond(to_other_core, other_core, keep, units)
    late_branches = [
        functools.partial(late_branch, mask) for mask in range(0, lax.axis_size("replica"), 2)
    ]
    late_units = lax.cond(
        more[0] == 1,
        lambda value: lax.cond(
            to_other_core, swapped(1), keep, lax.switch(chip_mask, late_branches, value)
        ),
        keep,
        late_payload,
    )
    last_branches = [
        functools.partial(last_branch, mask) for mask in range(1, lax.axis_size("replica"))
    ]
    second, cache, down, up = lax.switch(
        mask - 1,
        last_branches,
        tables,
        replica_pair_mask,
        units,
        late_units,
        second,
        leaving,
        factors,
    )
    cache = cache.reshape(MOVING_REQUESTS, MAXB * BLOCK_TOKENS, 2, HEAD_WIDTH)
    return first, second, cache, down, up


def solution(mesh):
    placed = (
        P("replica", "tensor"),
        P("replica", None, "tensor"),
        P("replica", "tensor"),
        P("replica", None, "tensor"),
        P("replica", None, None, "tensor"),
        P(),
        P(),
        P(),
        P(),
        P(),
        P(),
        P("replica", "tensor", None),
        P("replica", None, "tensor"),
        P("tensor", None),
    )
    return jax.shard_map(
        shards,
        mesh=mesh,
        in_specs=placed,
        out_specs=(
            P("replica", "tensor"),
            P("replica", "tensor"),
            P("replica", None, None, "tensor"),
            P("replica", "tensor", None),
            P("replica", None, "tensor"),
        ),
        check_vma=False,
    )
```
